256 devices in a mesh: wide: 32 (over x, y, core), narrow: 8 (over z).
Axes of the slice: x: 4, y: 4, z: 8, core: 2. Of those that a mesh axis runs over, the one named last changes fastest.
Arguments:
- pair_tokens: bfloat16 [256, 2, 128, 768], P(('wide', 'narrow')), may hold values from -6 to 6
- expert_ids: int32 [256, 256, 2], P(('wide', 'narrow')), may hold values from 0 to 31, all different within a row; in each aligned block of 256 rows (0 to 255, 256 to 511, ..., all dimensions but the last counted through in order) at most 17 rows name the same one
- positive: int32 [256], replicated, may hold values from 0 to 255, each once
- w_qkv: bfloat16 [768, 2304], replicated, may hold values from -0.21875 to 0.21875
- w_out: bfloat16 [768, 768], replicated, may hold values from -0.21875 to 0.21875
- w_router: bfloat16 [768, 32], replicated, may hold values from -0.21875 to 0.21875
- w_up: bfloat16 [32, 768, 3072], P('wide', None, 'narrow'), may hold values from -0.21875 to 0.21875
- w_down: bfloat16 [32, 3072, 768], P('wide', 'narrow'), may hold values from -0.109375 to 0.109375
Outputs:
- grad_up: float32 [32, 768, 3072], P('wide', None, 'narrow')
- grad_down: float32 [32, 3072, 768], P('wide', 'narrow')
The draws below stay inside these ranges and needn't reach their ends.
Inputs may be any that keep to these rules, and one draw needn't show every extreme that they name: `expert_ids`: the two experts of a token differ. Among the 256 tokens of one device no expert is named more than 17 times, and in every draw some device names some expert exactly 17 times. Each document is the positive of exactly one query.
All inputs are finite; a program needn't handle non-finite values.
Results may differ from the reference program's by a relative error of at most 0.023.
Values may be sent and summed in bfloat16 or wider, within the bound.
A program may use at most 128 MiB of HBM per device.

```python
import math
import jax
import jax.numpy as jnp
import numpy as np
from jax import lax

D = 768
FF = 3072
HEADS = 12
HEAD_DIM = 64
SEQ = 128
TOK_DEV = 256
EXPERTS = 32
CAP = 17
PAIRS = 256
N_WIDE = 32
N_NARROW = 8


def level_of(own_key, dims, cuts, smallest, top_value):
    factor_of, own = 1.0, jax.random.fold_in(own_key, 6)
    for position, parts in cuts:
        steps = jnp.exp(jax.random.uniform(jax.random.fold_in(own, position), (parts,), jnp.float32, smallest / len(cuts), top_value / len(cuts)))
        factor_of = factor_of * jnp.repeat(steps, dims[position] // parts).reshape([-1 if axis == position else 1 for axis in range(len(dims))])
    return factor_of


def deal_out(own_key, own, number, rows, number_of, top, most, slope):
    order = jax.random.permutation(own_key, number_of)
    crowded, usual = shares(number_of, rows * top, most, slope, True), shares(number_of, rows * top, most, slope, False)
    places = jnp.arange(number_of)

    def named(tallies, rotation):
        used = int((tallies > 0).sum())
        fixed = max(1, used // 4)
        shifted = fixed + (places - fixed + rotation * (used - fixed)) % max(1, number_of - fixed)
        return jnp.zeros((number_of,), jnp.int32).at[order[jnp.where(places < fixed, places, shifted)]].set(jnp.asarray(tallies, jnp.int32))

    tallies = jnp.where(number % 4 == 0, named(crowded, number // 4), named(usual, number - number // 4 - 1))
    mixed = jax.random.permutation(jax.random.fold_in(own, 3), number_of)
    donor, receiver = mixed[0:number_of // 2 * 2:2], mixed[1:number_of // 2 * 2:2]
    margin = jnp.minimum(tallies[donor] - 1, most - tallies[receiver]) // 2
    margin = jnp.where((donor == order[0]) | (receiver == order[0]) | (tallies[receiver] == 0), 0, jnp.maximum(margin, 0))
    shifted = jax.random.randint(jax.random.fold_in(own, 4), (number_of // 2,), 0, 1 << 20) % (margin + 1)
    tallies = tallies.at[donor].add(-shifted).at[receiver].add(shifted)
    items = jnp.searchsorted(jnp.cumsum(tallies), jnp.arange(rows * top), side="right").astype(jnp.int32)
    grid = items.reshape(top, rows).T
    grid = grid[jax.random.permutation(jax.random.fold_in(own, 1), rows)]
    rotation = jax.random.randint(jax.random.fold_in(own, 2), (rows, 1), 0, top)
    return jnp.take_along_axis(grid, (jnp.arange(top)[None, :] + rotation) % top, axis=1)


def shares(number_of, total, most, slope, full):
    portions = [(1 << 20) // math.isqrt(grade ** slope) + 1 for grade in range(1, number_of + 1)]
    largest = most if full else min(most, max(-(-total // number_of), total * portions[0] // sum(portions)))
    least = 1 if total - largest >= number_of - 1 else 0
    counts, spare = [largest] + [least] * (number_of - 1), total - largest - least * (number_of - 1)
    while spare > 0:
        movable = [i for i in range(1, number_of) if counts[i] < largest] or [i for i in range(1, number_of) if counts[i] < most]
        pool, budget = sum([portions[i] for i in movable]), spare
        for i in movable:
            addition = min(most - counts[i], max(1, budget * portions[i] // pool), spare)
            counts[i] = counts[i] + addition
            spare = spare - addition
    return np.array(counts)


def gaussian(own_key, extent, scale, most, cuts=(), kind=jnp.bfloat16):
    gain = level_of(own_key, extent, cuts, -0.22, 0.18) if cuts else 1.0
    array = jax.random.normal(own_key, extent, jnp.float32) * scale * gain
    return jnp.minimum(jnp.maximum(array, -most), most).astype(kind)


def setup_inputs(seed: int = 0) -> dict:
    seeds = jax.random.split(jax.random.key(seed), 9)
    pair_tokens = gaussian(seeds[0], (PAIRS, 2, SEQ, D), 1.0, 6.0, ((0, 256),))
    expert_ids_keys = jax.random.split(jax.random.fold_in(seeds[1], 1), PAIRS * (2 * SEQ) // TOK_DEV)
    expert_ids_turns = jax.random.permutation(jax.random.fold_in(seeds[1], 3), PAIRS * (2 * SEQ) // TOK_DEV)
    expert_ids = jax.vmap(lambda own, number: deal_out(jax.random.fold_in(seeds[1], 2), own, number, TOK_DEV, EXPERTS, 2, CAP, 1))(expert_ids_keys, expert_ids_turns).reshape((PAIRS, 2 * SEQ, 2))
    positive = jax.random.permutation(seeds[2], PAIRS).astype(jnp.int32)
    w_qkv = gaussian(seeds[3], (D, 3 * D), D ** -0.5, 0.21875)
    w_out = gaussian(seeds[4], (D, D), D ** -0.5, 0.21875)
    w_router = gaussian(seeds[5], (D, EXPERTS), D ** -0.5, 0.21875)
    w_up = gaussian(seeds[6], (EXPERTS, D, FF), D ** -0.5, 0.21875, ((0, 32), (2, 8)))
    w_down = gaussian(seeds[7], (EXPERTS, FF, D), FF ** -0.5, 0.109375, ((0, 32), (1, 8)))
    return {"pair_tokens": pair_tokens, "expert_ids": expert_ids, "positive": positive, "w_qkv": w_qkv, "w_out": w_out, "w_router": w_router, "w_up": w_up, "w_down": w_down}


epsilon = 1e-06
inverse_softmax_warmth = 20.0
loss_scale = 64.0

def rms_scaled(values):
    return values * lax.rsqrt(lax.optimization_barrier(jnp.mean(values * values, axis=-1, keepdims=True)) + epsilon)

def attention_block(tokens, w_qkv, w_out):
    count = tokens.shape[0]
    width = tokens.shape[1]
    normed = rms_scaled(tokens.astype(jnp.float32)).astype(jnp.bfloat16)
    project = jnp.dot(normed, w_qkv, preferred_element_type=jnp.float32)
    project = project.reshape(count // SEQ, SEQ, 3, HEADS, HEAD_DIM)
    query = rms_scaled(project[:, :, 0]).astype(jnp.bfloat16)
    keys_normed = rms_scaled(project[:, :, 1]).astype(jnp.bfloat16)
    values_cast = project[:, :, 2].astype(jnp.bfloat16)
    cosine_logit_matrix = jnp.einsum('sqhe,skhe->shqk', query.astype(jnp.float32), keys_normed.astype(jnp.float32)) / math.sqrt(HEAD_DIM)
    weights = jnp.exp(cosine_logit_matrix)
    weights = (weights / lax.optimization_barrier(jnp.sum(weights, axis=-1, keepdims=True))).astype(jnp.bfloat16)
    mixed = jnp.einsum('shqk,skhe->sqhe', weights.astype(jnp.float32), values_cast.astype(jnp.float32))
    mixed = mixed.astype(jnp.bfloat16).reshape(count, width)
    update = jnp.dot(mixed, w_out, preferred_element_type=jnp.float32)
    return (tokens.astype(jnp.float32) + update).astype(jnp.bfloat16)

def gate_pair(logits, picks):
    experts = logits.shape[-1]
    onehot = (picks[:, :, None] == jnp.arange(experts, dtype=jnp.int32)[None, None, :]).astype(jnp.float32)
    chosen_logits = lax.optimization_barrier(jnp.sum(onehot * logits[:, None, :], axis=-1))
    first = jax.nn.sigmoid(chosen_logits[:, 0] - chosen_logits[:, 1])
    return jnp.stack([first, 1.0 - first], axis=1)

def slot_positions(picks, experts, capacity):
    flat = picks.reshape(-1).astype(jnp.int32)
    onehot = (flat[:, None] == jnp.arange(experts, dtype=jnp.int32)[None, :]).astype(jnp.int32)
    earlier = jnp.cumsum(onehot, axis=0) - onehot
    return flat * capacity + lax.optimization_barrier(jnp.sum(earlier * onehot, axis=1)).astype(jnp.int32)

def reference(pair_tokens, expert_ids, positive, w_qkv, w_out, w_router, w_up, w_down):
    devices = N_WIDE * N_NARROW
    total = devices * TOK_DEV
    blocks_in = pair_tokens.reshape(devices, TOK_DEV, D)
    picks_in = expert_ids.reshape(devices, TOK_DEV, 2)

    def front(pieces):
        block, picks = pieces
        hidden_state = attention_block(block, w_qkv, w_out)
        normed = rms_scaled(hidden_state.astype(jnp.float32)).astype(jnp.bfloat16)
        logits = jnp.dot(normed, w_router, preferred_element_type=jnp.float32)
        gates = gate_pair(logits, picks)
        destination = slot_positions(picks, EXPERTS, CAP)
        return (hidden_state, normed, gates, destination)
    hidden_state, normed, gates, destination = lax.map(front, (blocks_in, picks_in))
    device_index = jnp.arange(devices, dtype=jnp.int32)[:, None]
    global_row = destination // CAP * (devices * CAP) + device_index * CAP + destination % CAP
    source = device_index * TOK_DEV + jnp.arange(2 * TOK_DEV, dtype=jnp.int32)[None, :] // 2
    table = jnp.full((EXPERTS * devices * CAP,), total, dtype=jnp.int32)
    table = table.at[global_row.reshape(-1)].set(source.reshape(-1).astype(jnp.int32))
    table = table.reshape(EXPERTS, devices * CAP)
    padded = jnp.concatenate([normed.reshape(total, D), jnp.zeros((1, D), normed.dtype)], axis=0)
    block_width = FF // N_NARROW

    def expert_forward(pieces):
        index, up_weight, down_weight = pieces
        slot_rows = padded[index]
        pre_act = jnp.dot(slot_rows, up_weight, preferred_element_type=jnp.float32)
        activated = jax.nn.gelu(pre_act).astype(jnp.bfloat16)
        split = activated.reshape(-1, N_NARROW, block_width).astype(jnp.float32)
        downs = down_weight.reshape(N_NARROW, block_width, D).astype(jnp.float32)
        partial_value = jnp.einsum('rnf,nfd->nrd', split, downs)
        rounded = lax.optimization_barrier(partial_value.astype(jnp.bfloat16))
        return lax.optimization_barrier(jnp.sum(rounded.astype(jnp.float32), axis=0)).astype(jnp.bfloat16)
    expert_out = lax.map(expert_forward, (table, w_up, w_down)).reshape(EXPERTS * devices * CAP, D)
    picked = expert_out[global_row.reshape(-1)].reshape(devices, TOK_DEV, 2, D)
    mixed = hidden_state.astype(jnp.float32) + lax.optimization_barrier(jnp.sum(gates[:, :, :, None] * picked.astype(jnp.float32), axis=2))
    pooled = lax.optimization_barrier(jnp.mean(mixed.reshape(PAIRS, 2, SEQ, D), axis=2))
    length = jnp.sqrt(lax.optimization_barrier(jnp.sum(pooled * pooled, axis=-1, keepdims=True)) + epsilon)
    unit = pooled / length
    search_unit_vector = unit[:, 0]
    passage_unit_vector = unit[:, 1]
    cosine_logit_matrix = jnp.dot(search_unit_vector, passage_unit_vector.T, precision=lax.Precision.HIGHEST) * inverse_softmax_warmth
    probs = jnp.exp(cosine_logit_matrix)
    probs = probs / lax.optimization_barrier(jnp.sum(probs, axis=1, keepdims=True))
    target = (positive[:, None] == jnp.arange(PAIRS, dtype=jnp.int32)[None, :]).astype(jnp.float32)
    logit_excess_matrix = (probs - target) * loss_scale
    search_embedding_adjoint = jnp.dot(logit_excess_matrix, passage_unit_vector, precision=lax.Precision.HIGHEST) * inverse_softmax_warmth
    passage_embedding_adjoint = jnp.dot(logit_excess_matrix.T, search_unit_vector, precision=lax.Precision.HIGHEST) * inverse_softmax_warmth
    unit_grad = jnp.stack([search_embedding_adjoint, passage_embedding_adjoint], axis=1)
    pooled_grad = (unit_grad - unit * lax.optimization_barrier(jnp.sum(unit * unit_grad, axis=-1, keepdims=True))) / length
    token_grad = jnp.broadcast_to((pooled_grad / SEQ)[:, :, None, :], (PAIRS, 2, SEQ, D)).reshape(devices, TOK_DEV, D)
    cotangent = (gates[:, :, :, None] * token_grad[:, :, None, :]).astype(jnp.bfloat16).reshape(-1, D)
    cot_table = jnp.zeros((EXPERTS * devices * CAP, D), jnp.bfloat16).at[global_row.reshape(-1)].set(cotangent)
    cot_table = cot_table.reshape(EXPERTS, devices * CAP, D)

    def expert_backward(pieces):
        index, up_weight, down_weight, grad_rows = pieces
        slot_rows = padded[index]
        pre_act = jnp.dot(slot_rows, up_weight, preferred_element_type=jnp.float32)
        activated = jax.nn.gelu(pre_act).astype(jnp.bfloat16)
        down_grad = jnp.dot(activated.T, grad_rows, preferred_element_type=jnp.float32)
        act_grad = jnp.dot(grad_rows, down_weight.T, preferred_element_type=jnp.float32)
        unused, pullback = jax.vjp(jax.nn.gelu, pre_act)
        pre_grad = pullback(act_grad)[0].astype(jnp.bfloat16)
        up_grad = jnp.dot(slot_rows.T, pre_grad, preferred_element_type=jnp.float32)
        return (up_grad, down_grad)
    grad_up, grad_down = lax.map(expert_backward, (table, w_up, w_down, cot_table))
    return (grad_up, grad_down)
```

```python
import functools

import jax
import jax.numpy as jnp
from jax import lax
from jax.experimental import pallas as pl
from jax.experimental.pallas import tpu as pltpu
from jax.sharding import PartitionSpec as P

D = 768
FB = 384
SEQ = 128
TOK = 256
NE = 32
MAIN = 16
CHUNKS = 4
EPS = 1e-06
WARMTH = 20.0
LOSS_SCALE = 64.0
VMEM_BYTES = 56 * 2**20
MESH = pl.DeviceIdType.MESH
HIGHEST = lax.Precision.HIGHEST
F32, BF16, I32 = jnp.float32, jnp.bfloat16, jnp.int32


def mm(a, b, ca=1, cb=0, precision=None):
    return lax.dot_general(
        a, b, (((ca,), (cb,)), ((), ())), precision=precision, preferred_element_type=F32
    )


def iota(shape, axis):
    return lax.broadcasted_iota(I32, shape, axis)


def onehot(condition):
    return jnp.where(condition, 1.0, 0.0).astype(BF16)


def rms(v):
    return v * lax.rsqrt(jnp.mean(v * v, axis=-1, keepdims=True) + EPS)


def front_kernel(x_ref, ids_ref, wqkv_ref, wout_ref, wr_ref, main_ref, side_ref, mean_ref, mixed):
    normed = rms(x_ref[...].astype(F32)).astype(BF16)
    wide = 256
    same_head = onehot(iota((wide, wide), 0) // 64 == iota((wide, wide), 1) // 64)
    low = iota((SEQ, 128), 1) < 64
    ones = jnp.ones((SEQ, 128), BF16)

    def head_rms(v):
        square = v * v
        high = square.astype(BF16)
        rest = (square - high.astype(F32)).astype(BF16)
        mean = (mm(high, same_head) + mm(rest, same_head)) * (1.0 / 64.0)
        return (v * lax.rsqrt(mean + EPS)).astype(BF16)

    for block in range(D // wide):
        at = block * wide
        q = head_rms(mm(normed, wqkv_ref[:, at : at + wide]))
        k = head_rms(mm(normed, wqkv_ref[:, D + at : D + at + wide]))
        v = mm(normed, wqkv_ref[:, 2 * D + at : 2 * D + at + wide]).astype(BF16)
        for s in range(TOK // SEQ):
            rows = slice(s * SEQ, (s + 1) * SEQ)
            for c in range(wide // 128):
                lanes = slice(c * 128, (c + 1) * 128)
                qc, kc = q[rows, lanes], k[rows, lanes]
                values = jnp.concatenate([v[rows, lanes], ones], axis=1)
                heads = []
                for half in range(2):
                    qh = jnp.where(low if half == 0 else ~low, qc, jnp.zeros_like(qc))
                    weights = jnp.exp(mm(qh, kc, 1, 1) * 0.125).astype(BF16)
                    both = mm(weights, values)
                    heads.append(both[:, :128] / both[:, 128:])
                mixed[rows, at + c * 128 : at + (c + 1) * 128] = jnp.where(
                    low, heads[0], heads[1]
                ).astype(BF16)

    h = (x_ref[...].astype(F32) + mm(mixed[...], wout_ref[...])).astype(BF16).astype(F32)
    mean_q = jnp.mean(h[:SEQ], axis=0, keepdims=True)
    mean_d = jnp.mean(h[SEQ:], axis=0, keepdims=True)
    mean_ref[...] = jnp.where(
        iota((8, D), 0) == 0, mean_q, jnp.where(iota((8, D), 0) == 1, mean_d, 0.0)
    )
    z = rms(h).astype(BF16)

    logits = mm(wr_ref[...], z, 0, 1)
    names = iota((TOK, NE), 1)
    named = onehot((ids_ref[:, 0:1] == names) | (ids_ref[:, 1:2] == names))
    row, col = iota((TOK, TOK), 0), iota((TOK, TOK), 1)
    picked = mm(named, jnp.concatenate([onehot(row == col), onehot(row < col)], axis=1), 0, 0)
    here = picked[:, :TOK] > 0.5
    rank = jnp.where(here, picked[:, TOK:], -1.0)
    both_logits = jnp.sum(jnp.where(here, logits, 0.0), axis=0, keepdims=True)
    gate = jnp.where(here, 1.0 / (1.0 + jnp.exp(both_logits - 2.0 * logits)), 0.0)

    spread = onehot(iota((NE * MAIN, NE), 0) // MAIN == iota((NE * MAIN, NE), 1))
    slot = (iota((NE * MAIN, TOK), 0) % MAIN).astype(F32)
    main_ref[...] = mm(onehot(mm(spread, rank.astype(BF16)) == slot), z).astype(BF16)

    extra = mm(onehot(rank == float(MAIN)), z).astype(BF16)
    lane = iota((NE, 128), 1)
    gates_q = jnp.zeros((NE, 128), F32)
    gates_d = jnp.zeros((NE, 128), F32)
    for s in range(MAIN + 1):
        chosen = jnp.where(rank == float(s), gate, 0.0)
        gates_q = jnp.where(lane == s, jnp.sum(chosen[:, :SEQ], axis=1, keepdims=True), gates_q)
        gates_d = jnp.where(lane == s, jnp.sum(chosen[:, SEQ:], axis=1, keepdims=True), gates_d)
    parts = [extra[:, c * 128 : (c + 1) * 128] for c in range(D // 128)]
    stacked = jnp.concatenate(parts + [gates_q.astype(BF16), gates_d.astype(BF16)], axis=0)
    r, c = iota((8 * NE, 8 * NE), 0), iota((8 * NE, 8 * NE), 1)
    side_ref[...] = mm(onehot(r == (c % NE) * 8 + c // NE), stacked)


def front(tokens, ids, w_qkv, w_out, w_router):
    return pl.pallas_call(
        front_kernel,
        out_shape=(
            jax.ShapeDtypeStruct((NE * MAIN, D), BF16),
            jax.ShapeDtypeStruct((8 * NE, 128), F32),
            jax.ShapeDtypeStruct((8, D), F32),
        ),
        scratch_shapes=[pltpu.VMEM((TOK, D), BF16)],
        compiler_params=pltpu.CompilerParams(vmem_limit_bytes=VMEM_BYTES),
        name="attention_and_slots",
    )(tokens, ids, w_qkv, w_out, w_router)


def dispatch_kernel(nw, nz, main_ref, side_ref, omain, oside, s1, r1, s2, r2):
    w, z = lax.axis_index("wide"), lax.axis_index("narrow")
    right, left = lax.rem(z + 1, nz), lax.rem(z + nz - 1, nz)
    hops, size = nz // 2, nw // CHUNKS

    barrier = pltpu.get_barrier_semaphore()

    def greet(d, carry):
        pl.semaphore_signal(
            barrier, inc=1, device_id=(lax.rem(w + d, nw), z), device_id_type=MESH
        )
        return carry

    lax.fori_loop(1, nw, greet, 0)
    for neighbour in (left, right):
        pl.semaphore_signal(barrier, inc=1, device_id=(w, neighbour), device_id_type=MESH)
    pl.semaphore_wait(barrier, nw + 1)

    pairs = ((main_ref, omain), (side_ref, oside))

    def first(d, part):
        source, target = pairs[part]
        peer = lax.rem(w + d, nw)
        return pltpu.make_async_remote_copy(
            src_ref=source.at[peer],
            dst_ref=target.at[z, w],
            send_sem=s1.at[part, d],
            recv_sem=r1.at[part, d],
            device_id=(peer, z),
            device_id_type=MESH,
        )

    def send(d, carry):
        for part in range(2):
            first(d, part).start()
        return carry

    for part in range(2):
        source, target = pairs[part]
        pltpu.make_async_copy(source.at[w], target.at[z, w], r1.at[part, 0]).start()
    lax.fori_loop(1, nw, send, 0)

    def arrived(c):
        def one(i, carry):
            origin = c * size + i
            d = lax.rem(w - origin + nw, nw)
            for part in range(2):
                source, target = pairs[part]
                pltpu.make_async_copy(
                    source.at[origin], target.at[z, origin], r1.at[part, d]
                ).wait()
            return carry

        lax.fori_loop(0, size, one, 0)

    def step(way, hop, c, part):
        plane = lax.rem(z - (hop - 1) + nz, nz) if way == 0 else lax.rem(z + (hop - 1), nz)
        block = pairs[part][1].at[plane, pl.ds(c * size, size)]
        return pltpu.make_async_remote_copy(
            src_ref=block,
            dst_ref=block,
            send_sem=s2.at[way, hop - 1, c, part],
            recv_sem=r2.at[way, hop - 1, c, part],
            device_id=(w, right if way == 0 else left),
            device_id_type=MESH,
        )

    def travels(way, hop, c):
        return hop < hops or (c < CHUNKS // 2) == (way == 0)

    for hop in range(hops + 1):
        for c in range(CHUNKS):
            if hop == 0:
                arrived(c)
            for way in range(2):
                if hop > 0 and travels(way, hop, c):
                    for part in range(2):
                        step(way, hop, c, part).wait_recv()
                if hop < hops and travels(way, hop + 1, c):
                    for part in range(2):
                        step(way, hop + 1, c, part).start()

    def drain(d, carry):
        for part in range(2):
            first(d, part).wait_send()
        return carry

    lax.fori_loop(1, nw, drain, 0)
    for hop in range(1, hops + 1):
        for c in range(CHUNKS):
            for way in range(2):
                if travels(way, hop, c):
                    for part in range(2):
                        step(way, hop, c, part).wait_send()


def dispatch(main, side):
    nw, nz = lax.axis_size("wide"), lax.axis_size("narrow")
    anywhere = pl.BlockSpec(memory_space=pl.ANY)
    return pl.pallas_call(
        functools.partial(dispatch_kernel, nw, nz),
        out_shape=(
            jax.ShapeDtypeStruct((nz,) + main.shape, main.dtype),
            jax.ShapeDtypeStruct((nz,) + side.shape, side.dtype),
        ),
        in_specs=[anywhere, anywhere],
        out_specs=(anywhere, anywhere),
        scratch_shapes=[
            pltpu.SemaphoreType.DMA((2, nw)),
            pltpu.SemaphoreType.DMA((2, nw)),
            pltpu.SemaphoreType.DMA((2, nz // 2, CHUNKS, 2)),
            pltpu.SemaphoreType.DMA((2, nz // 2, CHUNKS, 2)),
        ],
        compiler_params=pltpu.CompilerParams(collective_id=0, has_side_effects=True),
        name="dispatch_rows",
    )(main, side)


def unpack_side(side):
    r, c = iota((8 * NE, 8 * NE), 0), iota((8 * NE, 8 * NE), 1)
    ordered = mm(onehot(c == (r % NE) * 8 + r // NE), side.astype(BF16))
    extra = jnp.concatenate(
        [ordered[k * NE : (k + 1) * NE] for k in range(D // 128)], axis=1
    ).astype(BF16)
    repeat = onehot(iota((128, NE * MAIN), 0) == iota((128, NE * MAIN), 1) % MAIN)
    own = iota((NE, NE * MAIN), 1) // MAIN == iota((NE, NE * MAIN), 0)
    diagonal = iota((NE, NE), 0) == iota((NE, NE), 1)
    gates, gates_extra = [], []
    for k in (6, 7):
        g = ordered[k * NE : (k + 1) * NE]
        gates.append(jnp.where(own, mm(g.astype(BF16), repeat), 0.0))
        gates_extra.append(jnp.where(diagonal, g[:, MAIN : MAIN + 1], 0.0))
    return (
        extra,
        jnp.concatenate(gates, axis=0).astype(BF16),
        jnp.concatenate(gates_extra, axis=0).astype(BF16),
    )


def gelu_and_slope(x):
    a, b = 0.7978845608028654, 0.044715
    square = x * x
    t = jnp.tanh(a * x * (1.0 + b * square))
    half = 0.5 * (1.0 + t)
    slope = half + 0.5 * x * (1.0 - t * t) * (a * (1.0 + 3.0 * b * square))
    return (x * half).astype(BF16), slope.astype(BF16)


def sequence_order(transposed):
    n = 16 * NE
    a, b = (1, 0) if transposed else (0, 1)
    r, c = iota((n, n), a), iota((n, n), b)
    return onehot(c == (r % 8) * (2 * NE) + ((r // 8) % 2) * NE + r // 16)


def expert_kernel(main_ref, side_ref, up_ref, down_ref, slope_ref, slope_x_ref, acts_ref, part_ref, acts):
    plane = pl.program_id(0)
    extra, gates, gates_extra = unpack_side(side_ref[0])
    act, slope = gelu_and_slope(mm(main_ref[0], up_ref[...]))
    act_x, slope_x = gelu_and_slope(mm(extra, up_ref[...]))
    slope_ref[0] = slope
    slope_x_ref[0] = slope_x
    acts[plane] = (mm(gates, act) + mm(gates_extra, act_x)).astype(BF16)

    @pl.when(plane == pl.num_programs(0) - 1)
    def _():
        ordered = mm(sequence_order(False), acts[...].reshape(16 * NE, FB)).astype(BF16)
        acts_ref[...] = ordered
        part_ref[...] = mm(ordered, down_ref[...]).astype(BF16)


def experts(main, side, up, down):
    nz = main.shape[0]
    whole = lambda shape: pl.BlockSpec(shape, lambda p: (0,) * len(shape))
    each = lambda shape: pl.BlockSpec((1,) + shape, lambda p: (p,) + (0,) * len(shape))
    return pl.pallas_call(
        expert_kernel,
        grid=(nz,),
        in_specs=[each((NE * MAIN, D)), each((8 * NE, 128)), whole((D, FB)), whole((FB, D))],
        out_specs=(
            each((NE * MAIN, FB)),
            each((NE, FB)),
            whole((16 * NE, FB)),
            whole((16 * NE, D)),
        ),
        out_shape=(
            jax.ShapeDtypeStruct((nz, NE * MAIN, FB), BF16),
            jax.ShapeDtypeStruct((nz, NE, FB), BF16),
            jax.ShapeDtypeStruct((16 * NE, FB), BF16),
            jax.ShapeDtypeStruct((16 * NE, D), BF16),
        ),
        scratch_shapes=[pltpu.VMEM((nz, 2 * NE, FB), BF16)],
        compiler_params=pltpu.CompilerParams(vmem_limit_bytes=VMEM_BYTES),
        name="expert_forward",
    )(main, side, up, down)


def pool_kernel(nw, nz, part_ref, mean_ref, out_ref, got, zsend, zgot, s1, r1, s2, r2, s3, r3):
    w, z = lax.axis_index("wide"), lax.axis_index("narrow")
    rows = part_ref.shape[1]
    barrier = pltpu.get_barrier_semaphore()

    def greet(d, carry):
        pl.semaphore_signal(
            barrier, inc=1, device_id=(lax.rem(w + d, nw), z), device_id_type=MESH
        )
        return carry

    def greet_z(d, carry):
        pl.semaphore_signal(
            barrier, inc=1, device_id=(w, lax.rem(z + d, nz)), device_id_type=MESH
        )
        return carry

    lax.fori_loop(1, nw, greet, 0)
    lax.fori_loop(1, nz, greet_z, 0)
    pl.semaphore_wait(barrier, nw + nz - 2)

    def to_wide(source, target, sends, recvs, d):
        return pltpu.make_async_remote_copy(
            src_ref=source,
            dst_ref=target,
            send_sem=sends.at[d],
            recv_sem=recvs.at[d],
            device_id=(lax.rem(w + d, nw), z),
            device_id_type=MESH,
        )

    def scatter(d):
        return to_wide(part_ref.at[lax.rem(w + d, nw)], got.at[d], s1, r1, d)

    def across(d):
        return pltpu.make_async_remote_copy(
            src_ref=zsend,
            dst_ref=zgot.at[d],
            send_sem=s2.at[d],
            recv_sem=r2.at[d],
            device_id=(w, lax.rem(z + d, nz)),
            device_id_type=MESH,
        )

    def gather(d):
        return to_wide(out_ref.at[w], out_ref.at[w], s3, r3, d)

    def gathered(d):
        block = out_ref.at[lax.rem(w - d + nw, nw)]
        return to_wide(block, block, s3, r3, d)

    def each(count, act):
        def one(d, carry):
            act(d)
            return carry

        lax.fori_loop(1, count, one, 0)

    def summed(count, copy, buffer, start):
        def one(d, total):
            copy(d).wait_recv()
            return total + buffer[d].astype(F32)

        return lax.fori_loop(1, count, one, start)

    each(nw, lambda d: scatter(d).start())
    total = summed(nw, scatter, got, part_ref[w].astype(F32)) * (1.0 / SEQ)
    row = iota((rows, 1), 0)
    total = total + jnp.where(row == z, mean_ref[0:1], 0.0)
    total = total + jnp.where(row == z + rows // 2, mean_ref[1:2], 0.0)
    zsend[...] = total.astype(BF16)
    each(nz, lambda d: across(d).start())
    total = summed(nz, across, zgot, total)
    out_ref[w] = total.astype(out_ref.dtype)
    each(nw, lambda d: gather(d).start())
    each(nw, lambda d: gathered(d).wait_recv())
    each(nw, lambda d: scatter(d).wait_send())
    each(nz, lambda d: across(d).wait_send())
    each(nw, lambda d: gather(d).wait_send())


def pool(part, mean):
    nw, nz = lax.axis_size("wide"), lax.axis_size("narrow")
    rows = part.shape[1]
    wide_sems = [pltpu.SemaphoreType.DMA((nw,))] * 2
    vmem = pl.BlockSpec(memory_space=pltpu.VMEM)
    return pl.pallas_call(
        functools.partial(pool_kernel, nw, nz),
        out_shape=jax.ShapeDtypeStruct((nw, rows, part.shape[2]), F32),
        in_specs=[vmem, vmem],
        out_specs=vmem,
        scratch_shapes=[
            pltpu.VMEM(part.shape, BF16),
            pltpu.VMEM(part.shape[1:], BF16),
            pltpu.VMEM((nz,) + part.shape[1:], BF16),
            *wide_sems,
            pltpu.SemaphoreType.DMA((nz,)),
            pltpu.SemaphoreType.DMA((nz,)),
            *wide_sems,
        ],
        compiler_params=pltpu.CompilerParams(
            collective_id=1, has_side_effects=True, vmem_limit_bytes=VMEM_BYTES
        ),
        name="pooled_rows",
    )(part, mean)


def row_gradients(pooled, positive):
    pairs = 8 * NE
    query = pooled[:, :8].reshape(pairs, D)
    document = pooled[:, 8:].reshape(pairs, D)
    length_q = jnp.sqrt(jnp.sum(query * query, axis=-1, keepdims=True) + EPS)
    length_d = jnp.sqrt(jnp.sum(document * document, axis=-1, keepdims=True) + EPS)
    unit_q, unit_d = query / length_q, document / length_d
    weights = jnp.exp(mm(unit_q, unit_d, 1, 1, HIGHEST) * WARMTH)
    probs = weights / jnp.sum(weights, axis=1, keepdims=True)
    target = jnp.where(positive == iota((pairs, pairs), 1), 1.0, 0.0)
    excess = (probs - target) * (LOSS_SCALE * WARMTH)
    grad_q = mm(excess, unit_d, 1, 0, HIGHEST)
    grad_d = mm(excess, unit_q, 0, 0, HIGHEST)

    def back(unit, grad, length):
        inner = jnp.sum(unit * grad, axis=-1, keepdims=True)
        return ((grad - unit * inner) / (length * float(SEQ))).reshape(NE, 8, D)

    both = [back(unit_q, grad_q, length_q), back(unit_d, grad_d, length_d)]
    return jnp.concatenate(both, axis=1).reshape(16 * NE, D).astype(BF16)


def gradient_kernel(
    pooled_ref, positive_ref, acts_ref, down_ref, main_ref, side_ref, slope_ref, slope_x_ref,
    grad_up_ref, grad_down_ref, spread,
):
    plane = pl.program_id(0)

    @pl.when(plane == 0)
    def _():
        dy = row_gradients(pooled_ref[...], positive_ref[...])
        grad_down_ref[...] = mm(acts_ref[...], dy, 0, 0)
        back = mm(dy, down_ref[...], 1, 1).astype(BF16)
        spread[...] = (
            mm(sequence_order(True), back).astype(BF16).reshape(spread.shape)
        )
        grad_up_ref[...] = jnp.zeros_like(grad_up_ref)

    extra, gates, gates_extra = unpack_side(side_ref[0])
    back = spread[plane]
    dpre = (mm(gates, back, 0, 0) * slope_ref[0].astype(F32)).astype(BF16)
    dpre_x = (mm(gates_extra, back, 0, 0) * slope_x_ref[0].astype(F32)).astype(BF16)
    grad_up_ref[...] += mm(main_ref[0], dpre, 0, 0) + mm(extra, dpre_x, 0, 0)


def gradients(pooled, positive, acts, down, main, side, slope, slope_x):
    nz = main.shape[0]
    whole = lambda shape: pl.BlockSpec(shape, lambda p: (0,) * len(shape))
    each = lambda shape: pl.BlockSpec((1,) + shape, lambda p: (p,) + (0,) * len(shape))
    return pl.pallas_call(
        gradient_kernel,
        grid=(nz,),
        in_specs=[
            whole(pooled.shape),
            whole(positive.shape),
            whole(acts.shape),
            whole((FB, D)),
            each((NE * MAIN, D)),
            each((8 * NE, 128)),
            each((NE * MAIN, FB)),
            each((NE, FB)),
        ],
        out_specs=(whole((D, FB)), whole((FB, D))),
        out_shape=(
            jax.ShapeDtypeStruct((D, FB), F32),
            jax.ShapeDtypeStruct((FB, D), F32),
        ),
        scratch_shapes=[pltpu.VMEM((nz, 2 * NE, FB), BF16)],
        compiler_params=pltpu.CompilerParams(vmem_limit_bytes=VMEM_BYTES),
        name="expert_gradients",
    )(pooled, positive, acts, down, main, side, slope, slope_x)


def body(pair_tokens, expert_ids, positive, w_qkv, w_out, w_router, w_up, w_down):
    nz = lax.axis_size("narrow")
    main, side, mean = front(
        pair_tokens.reshape(TOK, D), expert_ids.reshape(TOK, 2), w_qkv, w_out, w_router
    )
    main, side = dispatch(main.reshape(NE, MAIN, D), side.reshape(NE, 8, 128))
    main = main.reshape(nz, NE * MAIN, D)
    side = side.reshape(nz, NE * 8, 128)
    slope, slope_x, acts, part = experts(main, side, w_up[0], w_down[0])
    pooled = pool(part.reshape(NE, 16, D), mean)
    grad_up, grad_down = gradients(
        pooled, positive.reshape(-1, 1), acts, w_down[0], main, side, slope, slope_x
    )
    return (grad_up[None], grad_down[None])


def solution(mesh):
    return jax.shard_map(
        body,
        mesh=mesh,
        in_specs=(
            P(("wide", "narrow"), None, None, None),
            P(("wide", "narrow"), None, None),
            P(),
            P(),
            P(),
            P(),
            P("wide", None, "narrow"),
            P("wide", "narrow", None),
        ),
        out_specs=(P("wide", None, "narrow"), P("wide", "narrow", None)),
        check_vma=False,
    )
```

```python
import functools

import jax
import jax.numpy as jnp
from jax import lax
from jax.experimental import pallas as pl
from jax.experimental.pallas import tpu as pltpu
from jax.sharding import PartitionSpec as P

D = 768
FB = 384
SEQ = 128
TOK = 256
NE = 32
MAIN = 16
ROW = D + 128
CHUNKS = 4
SIZE = NE // CHUNKS
CROWS = SIZE * MAIN
EPS = 1e-06
WARMTH = 20.0
LOSS_SCALE = 64.0
VMEM_BYTES = 56 * 2**20
MESH = pl.DeviceIdType.MESH
HIGHEST = lax.Precision.HIGHEST
F32, BF16, I32 = jnp.float32, jnp.bfloat16, jnp.int32


def mm(a, b, ca=1, cb=0, precision=None):
    return lax.dot_general(
        a, b, (((ca,), (cb,)), ((), ())), precision=precision, preferred_element_type=F32
    )


def iota(shape, axis):
    return lax.broadcasted_iota(I32, shape, axis)


def onehot(condition):
    return jnp.where(condition, 1.0, 0.0).astype(BF16)


def rms(v):
    return v * lax.rsqrt(jnp.mean(v * v, axis=-1, keepdims=True) + EPS)


def front(x_ref, ids_ref, wqkv_ref, wout_ref, wr_ref, blocks, mixed):
    normed = rms(x_ref[...].astype(F32)).astype(BF16)
    wide = 256
    same_head = onehot(iota((wide, wide), 0) // 64 == iota((wide, wide), 1) // 64)
    low = iota((SEQ, 128), 1) < 64
    ones = jnp.ones((SEQ, 128), BF16)

    def head_rms(v):
        square = v * v
        high = square.astype(BF16)
        rest = (square - high.astype(F32)).astype(BF16)
        mean = (mm(high, same_head) + mm(rest, same_head)) * (1.0 / 64.0)
        return (v * lax.rsqrt(mean + EPS)).astype(BF16)

    for block in range(D // wide):
        at = block * wide
        q = head_rms(mm(normed, wqkv_ref[:, at : at + wide]))
        k = head_rms(mm(normed, wqkv_ref[:, D + at : D + at + wide]))
        v = mm(normed, wqkv_ref[:, 2 * D + at : 2 * D + at + wide]).astype(BF16)
        for s in range(TOK // SEQ):
            rows = slice(s * SEQ, (s + 1) * SEQ)
            for c in range(wide // 128):
                lanes = slice(c * 128, (c + 1) * 128)
                qc, kc = q[rows, lanes], k[rows, lanes]
                values = jnp.concatenate([v[rows, lanes], ones], axis=1)
                heads = []
                for half in range(2):
                    qh = jnp.where(low if half == 0 else ~low, qc, jnp.zeros_like(qc))
                    weights = jnp.exp(mm(qh, kc, 1, 1) * 0.125).astype(BF16)
                    both = mm(weights, values)
                    heads.append(both[:, :128] / both[:, 128:])
                mixed[rows, at + c * 128 : at + (c + 1) * 128] = jnp.where(
                    low, heads[0], heads[1]
                ).astype(BF16)

    h = (x_ref[...].astype(F32) + mm(mixed[...], wout_ref[...])).astype(BF16).astype(F32)
    mean_q = jnp.mean(h[:SEQ], axis=0, keepdims=True)
    mean_d = jnp.mean(h[SEQ:], axis=0, keepdims=True)
    z = rms(h).astype(BF16)

    logits = mm(wr_ref[...], z, 1, 1)
    names = iota((NE, TOK), 0)
    here = (ids_ref[0:1, :] == names) | (ids_ref[1:2, :] == names)
    earlier = onehot(iota((TOK, TOK), 0) < iota((TOK, TOK), 1))
    rank = jnp.where(here, mm(onehot(here), earlier), -1.0)
    both_logits = jnp.sum(jnp.where(here, logits, 0.0), axis=0, keepdims=True)
    gate = jnp.where(here, 1.0 / (1.0 + jnp.exp(both_logits - 2.0 * logits)), 0.0)

    spread = onehot(iota((NE * MAIN, NE), 0) // MAIN == iota((NE * MAIN, NE), 1))
    slot = (iota((NE * MAIN, TOK), 0) % MAIN).astype(F32)
    main = mm(onehot(mm(spread, rank.astype(BF16)) == slot), z).astype(BF16)
    blocks[:, :, :D] = main.reshape(NE, MAIN, D)

    extra = mm(onehot(rank == float(MAIN)), z).astype(BF16)
    lane = iota((NE, 128), 1)
    gates_q = jnp.zeros((NE, 128), F32)
    gates_d = jnp.zeros((NE, 128), F32)
    for s in range(MAIN + 1):
        chosen = jnp.where(rank == float(s), gate, 0.0)
        gates_q = jnp.where(lane == s, jnp.sum(chosen[:, :SEQ], axis=1, keepdims=True), gates_q)
        gates_d = jnp.where(lane == s, jnp.sum(chosen[:, SEQ:], axis=1, keepdims=True), gates_d)
    parts = [extra[:, c * 128 : (c + 1) * 128] for c in range(D // 128)]
    stacked = jnp.concatenate(parts + [gates_q.astype(BF16), gates_d.astype(BF16)], axis=0)
    r, c = iota((NE * MAIN, 8 * NE), 0), iota((NE * MAIN, 8 * NE), 1)
    side = mm(onehot(c == (r % MAIN) * NE + r // MAIN), stacked).astype(BF16)
    blocks[:, :, D:] = side.reshape(NE, MAIN, 128)
    return mean_q, mean_d


def gelu_and_slope(x):
    a, b = 0.7978845608028654, 0.044715
    square = x * x
    t = jnp.tanh(a * x * (1.0 + b * square))
    half = 0.5 * (1.0 + t)
    slope = half + 0.5 * x * (1.0 - t * t) * (a * (1.0 + 3.0 * b * square))
    return (x * half).astype(BF16), slope.astype(BF16)


def expert_chunk(plane, c, rows, up_ref, turned, extras, slopes, gates, acts):
    q = plane * CHUNKS + c
    block = rows[plane, pl.ds(c * SIZE, SIZE)].reshape(CROWS, ROW)
    main = block[:, :D]
    turned[q] = main.T
    r, col = iota((128, CROWS), 0), iota((128, CROWS), 1)
    take = onehot((col == (r % MAIN) * MAIN + r // MAIN) & (r % MAIN < SIZE))
    side = mm(take, block[:, D:])
    extra = jnp.concatenate(
        [side[k * MAIN : (k + 1) * MAIN] for k in range(D // 128)], axis=1
    ).astype(BF16)
    extras[q] = extra
    own = jnp.concatenate([side[6 * MAIN : 6 * MAIN + SIZE], side[7 * MAIN : 7 * MAIN + SIZE]])
    wide = CROWS + 128
    s, j = iota((128, wide), 0), iota((128, wide), 1)
    repeat = onehot(s == jnp.where(j < CROWS, j % MAIN, MAIN))
    i, j = iota((2 * SIZE, wide), 0), iota((2 * SIZE, wide), 1)
    mine = jnp.where(j < CROWS, j // MAIN, j - CROWS) == i % SIZE
    gate = jnp.where(mine, mm(own.astype(BF16), repeat), 0.0).astype(BF16)
    gates[q] = gate
    act, slope = gelu_and_slope(mm(main, up_ref[...]))
    act_x, slope_x = gelu_and_slope(mm(extra, up_ref[...]))
    slopes[q, :CROWS] = slope
    slopes[q, CROWS:] = slope_x
    total = mm(gate[:, :CROWS], act) + mm(gate[:, CROWS : CROWS + MAIN], act_x)
    acts[q] = total.astype(BF16)


def wide_of(i):
    return (i % (NE // 2)) * 2 + i // (NE // 2)


def sequence_order(transposed):
    n = 16 * NE
    a, b = (1, 0) if transposed else (0, 1)
    r, c = iota((n, n), a), iota((n, n), b)
    w = wide_of(r // 16)
    row = ((r % 8) * CHUNKS + w // SIZE) * 16 + ((r // 8) % 2) * 8 + w % SIZE
    return onehot(c == row)


def split(v):
    high = v.astype(BF16)
    return high, (v - high.astype(F32)).astype(BF16)


def row_gradients(pooled, positive):
    pairs = 8 * NE
    query = pooled[:, :8].reshape(pairs, D)
    document = pooled[:, 8:].reshape(pairs, D)
    query_b, document_b = query.astype(BF16), document.astype(BF16)
    inverse_q = lax.rsqrt(jnp.sum(query * query, axis=-1, keepdims=True) + EPS)
    inverse_d = lax.rsqrt(jnp.sum(document * document, axis=-1, keepdims=True) + EPS)
    squares = mm(jnp.ones((8, D), F32), document * document, 1, 1, HIGHEST)
    inverse_row = lax.rsqrt(squares[0:1] + EPS)
    weights = jnp.exp(mm(query_b, document_b, 1, 1) * (inverse_q * WARMTH) * inverse_row)
    probs = weights / jnp.sum(weights, axis=1, keepdims=True)

    def number(j):
        return wide_of(j // 8) * 8 + j % 8

    r, c = iota((pairs, pairs), 0), iota((pairs, pairs), 1)
    target = mm(onehot(number(r) == c), onehot(number(r) == positive), 1, 1)
    excess = (probs - target) * (LOSS_SCALE * WARMTH)
    high, rest = split(excess * inverse_row)
    grad_q = mm(high, document_b) + mm(rest, document_b)
    high, rest = split(excess * inverse_q)
    grad_d = mm(high, query_b, 0, 0) + mm(rest, query_b, 0, 0)

    def back(row, grad, inverse):
        unit = row * inverse
        inner = jnp.sum(unit * grad, axis=-1, keepdims=True)
        return ((grad - unit * inner) * (inverse * (1.0 / SEQ))).reshape(NE, 8, D)

    both = [back(query, grad_q, inverse_q), back(document, grad_d, inverse_d)]
    return jnp.concatenate(both, axis=1).reshape(16 * NE, D).astype(BF16)


def each(start, stop, act):
    def one(i, carry):
        act(i)
        return carry

    lax.fori_loop(start, stop, one, 0)


def step_kernel(
    nw, nz,
    x_ref, ids_ref, positive_ref, wqkv_ref, wout_ref, wr_ref, up_ref, down_ref,
    grad_up_ref, grad_down_ref,
    blocks, mixed, rows, turned, extras, slopes, gates, acts, spread, dpre, dpre_x,
    ordered, part, lent, half, got, zsend, zgot, pooled,
    s1, r1, s2, r2, sem_core, s3, r3, s4, r4, s5, r5, s6, r6,
):
    w, z = lax.axis_index("wide"), lax.axis_index("narrow")
    right, left = lax.rem(z + 1, nz), lax.rem(z + nz - 1, nz)
    hops, chips = nz // 2, nw // 2
    chip, core = w // 2, lax.rem(w, 2)
    sibling = w + 1 - 2 * core

    barrier = pltpu.get_barrier_semaphore()

    def greet(peer):
        pl.semaphore_signal(barrier, inc=1, device_id=peer, device_id_type=MESH)

    each(1, nw, lambda d: greet((lax.rem(w + d, nw), z)))
    each(1, nz, lambda d: greet((w, lax.rem(z + d, nz))))

    mean_q, mean_d = front(x_ref, ids_ref, wqkv_ref, wout_ref, wr_ref, blocks, mixed)

    pl.semaphore_wait(barrier, nw + nz - 2)

    def copy(source, target, send, receive, peer):
        return pltpu.make_async_remote_copy(
            src_ref=source, dst_ref=target, send_sem=send, recv_sem=receive,
            device_id=peer, device_id_type=MESH,
        )

    def first(d):
        peer = lax.rem(w + d, nw)
        return copy(blocks.at[peer], rows.at[z, w], s1.at[d], r1.at[d], (peer, z))

    pltpu.make_async_copy(blocks.at[w], rows.at[z, w], r1.at[0]).start()
    each(1, nw, lambda d: first(d).start())

    def arrived(c):
        def one(i):
            origin = c * SIZE + i
            pltpu.make_async_copy(
                blocks.at[origin], rows.at[z, origin], r1.at[lax.rem(w - origin + nw, nw)]
            ).wait()

        each(0, SIZE, one)

    def plane_at(way, hop):
        return lax.rem(z + nz - hop, nz) if way == 0 else lax.rem(z + hop, nz)

    def move(way, hop, c):
        block = rows.at[plane_at(way, hop - 1), pl.ds(c * SIZE, SIZE)]
        return copy(
            block, block, s2.at[way, hop - 1, c], r2.at[way, hop - 1, c],
            (w, right if way == 0 else left),
        )

    def work(plane, c):
        expert_chunk(plane, c, rows, up_ref, turned, extras, slopes, gates, acts)

    def home(c):
        arrived(c)
        for way in range(2):
            move(way, 1, c).start()
        work(z, c)

    each(0, CHUNKS, home)

    def both_ways(hop, c, onward):
        for way in range(2):
            move(way, hop, c).wait_recv()
            if way in onward:
                move(way, hop + 1, c).start()
        each(0, 2, lambda way: work(lax.rem(z + nz + (2 * way - 1) * hop, nz), c))

    each(0, (hops - 2) * CHUNKS, lambda i: both_ways(1 + i // CHUNKS, lax.rem(i, CHUNKS), (0, 1)))
    each(0, CHUNKS // 2, lambda c: both_ways(hops - 1, c, (0,)))
    each(CHUNKS // 2, CHUNKS, lambda c: both_ways(hops - 1, c, (1,)))

    def last(i):
        for way in range(2):
            move(way, hops, i + way * (CHUNKS // 2)).wait_recv()
        each(0, 2, lambda way: work(lax.rem(z + hops, nz), i + way * (CHUNKS // 2)))

    each(0, CHUNKS // 2, last)

    side = NE // 2 * 16
    ordered[...] = mm(sequence_order(False), acts[...].reshape(16 * NE, FB)).astype(BF16)

    def partial(which):
        return mm(ordered[pl.ds(pl.multiple_of(which * side, side), side)], down_ref[...])

    lent[...] = partial(1 - core).astype(BF16).reshape(lent.shape)
    swap = copy(lent, half, sem_core.at[0], sem_core.at[1], (sibling, z))
    swap.start()
    part[...] = partial(core).reshape(part.shape)
    swap.wait_recv()
    part[...] = part[...] + half[...].astype(F32)
    swap.wait_send()
    lent[...] = part[...].astype(BF16)

    def peer_chip(d):
        return lax.rem(chip + d, chips)

    def scatter(d):
        return copy(
            lent.at[peer_chip(d)], got.at[d], s3.at[d], r3.at[d], (peer_chip(d) * 2 + core, z)
        )

    def across(d):
        return copy(zsend, zgot.at[d], s4.at[d], r4.at[d], (w, lax.rem(z + d, nz)))

    def gather(d, origin):
        block = pooled.at[core, origin]
        return copy(block, block, s5.at[d], r5.at[d], (peer_chip(d) * 2 + core, z))

    def lend(d, origin, holder):
        block = pooled.at[holder, origin]
        return copy(block, block, s6.at[d], r6.at[d], (sibling, z))

    def summed(count, one_copy, buffer, start):
        def one(d, total):
            one_copy(d).wait_recv()
            return total + buffer[d].astype(F32)

        return lax.fori_loop(1, count, one, start)

    each(1, chips, lambda d: scatter(d).start())
    total = summed(chips, scatter, got, part[chip]) * (1.0 / SEQ)
    row = iota((16, 1), 0)
    total = total + jnp.where(row == z, mean_q, 0.0) + jnp.where(row == z + 8, mean_d, 0.0)
    zsend[...] = total.astype(BF16)
    each(1, nz, lambda d: across(d).start())
    pooled[core, chip] = summed(nz, across, zgot, total).astype(BF16)
    each(1, chips, lambda d: gather(d, chip).start())
    lend(0, chip, core).start()

    def pass_on(d):
        origin = lax.rem(chip - d + chips, chips)
        gather(d, origin).wait_recv()
        lend(d, origin, core).start()

    each(1, chips, pass_on)
    each(0, chips, lambda d: lend(d, lax.rem(chip - d + chips, chips), 1 - core).wait_recv())

    dy = row_gradients(pooled[...].reshape(NE, 16, D).astype(F32), positive_ref[...])
    grad_down_ref[...] = mm(ordered[...], dy, 0, 0)
    back = mm(dy, down_ref[...], 1, 1).astype(BF16)
    spread[...] = mm(sequence_order(True), back).astype(BF16).reshape(spread.shape)

    def before(q):
        gate, back = gates[q], spread[q]
        slope = slopes[q].astype(F32)
        dpre[q] = (mm(gate[:, :CROWS], back, 0, 0) * slope[:CROWS]).astype(BF16)
        dpre_x[q] = (
            mm(gate[:, CROWS : CROWS + MAIN], back, 0, 0) * slope[CROWS:]
        ).astype(BF16)

    each(0, nz * CHUNKS, before)
    extra_rows = nz * CHUNKS * MAIN
    grad_up_ref[...] = mm(
        extras[...].reshape(extra_rows, D), dpre_x[...].reshape(extra_rows, FB), 0, 0
    )

    def add(p):
        left_side = jnp.concatenate([turned[p * CHUNKS + c] for c in range(CHUNKS)], axis=1)
        right_side = dpre[pl.ds(p * CHUNKS, CHUNKS)].reshape(CHUNKS * CROWS, FB)
        grad_up_ref[...] += mm(left_side, right_side)

    each(0, nz, add)

    each(1, nw, lambda d: first(d).wait_send())
    for way in range(2):
        each(0, (hops - 1) * CHUNKS, lambda i: move(way, 1 + i // CHUNKS, lax.rem(i, CHUNKS)).wait_send())
        each(0, CHUNKS // 2, lambda i: move(way, hops, i + way * (CHUNKS // 2)).wait_send())
    each(1, chips, lambda d: scatter(d).wait_send())
    each(1, nz, lambda d: across(d).wait_send())
    each(1, chips, lambda d: gather(d, chip).wait_send())
    each(0, chips, lambda d: lend(d, lax.rem(chip - d + chips, chips), core).wait_send())


def body(pair_tokens, expert_ids, positive, w_qkv, w_out, w_router, w_up, w_down):
    nw, nz = lax.axis_size("wide"), lax.axis_size("narrow")
    chips, parts = nw // 2, nz * CHUNKS
    dma = pltpu.SemaphoreType.DMA
    vmem = pl.BlockSpec(memory_space=pltpu.VMEM)
    grad_up, grad_down = pl.pallas_call(
        functools.partial(step_kernel, nw, nz),
        out_shape=(
            jax.ShapeDtypeStruct((D, FB), F32),
            jax.ShapeDtypeStruct((FB, D), F32),
        ),
        in_specs=[vmem] * 8,
        out_specs=(vmem, vmem),
        scratch_shapes=[
            pltpu.VMEM((NE, MAIN, ROW), BF16),
            pltpu.VMEM((TOK, D), BF16),
            pltpu.VMEM((nz, nw, MAIN, ROW), BF16),
            pltpu.VMEM((parts, D, CROWS), BF16),
            pltpu.VMEM((parts, MAIN, D), BF16),
            pltpu.VMEM((parts, CROWS + MAIN, FB), BF16),
            pltpu.VMEM((parts, 2 * SIZE, CROWS + 128), BF16),
            pltpu.VMEM((parts, 2 * SIZE, FB), BF16),
            pltpu.VMEM((parts, 2 * SIZE, FB), BF16),
            pltpu.VMEM((parts, CROWS, FB), BF16),
            pltpu.VMEM((parts, MAIN, FB), BF16),
            pltpu.VMEM((16 * NE, FB), BF16),
            pltpu.VMEM((chips, 16, D), F32),
            pltpu.VMEM((chips, 16, D), BF16),
            pltpu.VMEM((chips, 16, D), BF16),
            pltpu.VMEM((chips, 16, D), BF16),
            pltpu.VMEM((16, D), BF16),
            pltpu.VMEM((nz, 16, D), BF16),
            pltpu.VMEM((2, chips, 16, D), BF16),
            dma((nw,)), dma((nw,)),
            dma((2, nz // 2, CHUNKS)), dma((2, nz // 2, CHUNKS)),
            dma((2,)),
            dma((chips,)), dma((chips,)),
            dma((nz,)), dma((nz,)),
            dma((chips,)), dma((chips,)),
            dma((chips,)), dma((chips,)),
        ],
        compiler_params=pltpu.CompilerParams(
            collective_id=0, has_side_effects=True, vmem_limit_bytes=VMEM_BYTES
        ),
        name="contrastive_step",
    )(
        pair_tokens.reshape(TOK, D),
        expert_ids.reshape(TOK, 2).T,
        positive.reshape(1, -1),
        w_qkv,
        w_out,
        w_router.T,
        w_up[0],
        w_down[0],
    )
    return (grad_up[None], grad_down[None])


def solution(mesh):
    return jax.shard_map(
        body,
        mesh=mesh,
        in_specs=(
            P(("wide", "narrow"), None, None, None),
            P(("wide", "narrow"), None, None),
            P(),
            P(),
            P(),
            P(),
            P("wide", None, "narrow"),
            P("wide", "narrow", None),
        ),
        out_specs=(P("wide", None, "narrow"), P("wide", "narrow", None)),
        check_vma=False,
    )
```

```python
import functools

import jax
import jax.numpy as jnp
from jax import lax
from jax.experimental import pallas as pl
from jax.experimental.pallas import tpu as pltpu
from jax.sharding import PartitionSpec as P

D = 768
FB = 384
SEQ = 128
TOK = 256
NE = 32
MAIN = 16
ROW = D + 128
CHUNKS = 4
AHEAD = 2
SIZE = NE // CHUNKS
CROWS = SIZE * MAIN
SROWS = SIZE * 8
STRIDE, UNSTRIDE = 11, 3
EPS = 1e-06
WARMTH = 20.0
LOSS_SCALE = 64.0
VMEM_BYTES = 56 * 2**20
MESH = pl.DeviceIdType.MESH
HIGHEST = lax.Precision.HIGHEST
F32, BF16, I32 = jnp.float32, jnp.bfloat16, jnp.int32


def mm(a, b, ca=1, cb=0, precision=None):
    return lax.dot_general(
        a, b, (((ca,), (cb,)), ((), ())), precision=precision, preferred_element_type=F32
    )


def iota(shape, axis):
    return lax.broadcasted_iota(I32, shape, axis)


def onehot(condition):
    return jnp.where(condition, 1.0, 0.0).astype(BF16)


def rms(v):
    return v * lax.rsqrt(jnp.mean(v * v, axis=-1, keepdims=True) + EPS)


def front(loads, x_ref, ids_ref, wqkv_ref, wout_ref, wr_ref, blocks, mixed):
    normed = rms(x_ref[...].astype(F32)).astype(BF16)
    wide = 256
    same_head = onehot(iota((wide, wide), 0) // 64 == iota((wide, wide), 1) // 64)
    low = iota((SEQ, 128), 1) < 64
    ones = jnp.ones((SEQ, 128), BF16)

    def head_rms(v):
        square = v * v
        high = square.astype(BF16)
        rest = (square - high.astype(F32)).astype(BF16)
        mean = (mm(high, same_head) + mm(rest, same_head)) * (1.0 / 64.0)
        return (v * lax.rsqrt(mean + EPS)).astype(BF16)

    for block in range(D // wide):
        at = block * wide
        loads.wait(block)
        q = head_rms(mm(normed, wqkv_ref[:, at : at + wide]))
        k = head_rms(mm(normed, wqkv_ref[:, D + at : D + at + wide]))
        v = mm(normed, wqkv_ref[:, 2 * D + at : 2 * D + at + wide]).astype(BF16)
        for s in range(TOK // SEQ):
            rows = slice(s * SEQ, (s + 1) * SEQ)
            for c in range(wide // 128):
                lanes = slice(c * 128, (c + 1) * 128)
                qc, kc = q[rows, lanes], k[rows, lanes]
                values = jnp.concatenate([v[rows, lanes], ones], axis=1)
                heads = []
                for half in range(2):
                    qh = jnp.where(low if half == 0 else ~low, qc, jnp.zeros_like(qc))
                    weights = jnp.exp(mm(qh, kc, 1, 1) * 0.125).astype(BF16)
                    both = mm(weights, values)
                    heads.append(both[:, :128] / both[:, 128:])
                mixed[rows, at + c * 128 : at + (c + 1) * 128] = jnp.where(
                    low, heads[0], heads[1]
                ).astype(BF16)

    loads.wait(D // wide)
    h = (x_ref[...].astype(F32) + mm(mixed[...], wout_ref[...])).astype(BF16).astype(F32)
    mean_q = jnp.mean(h[:SEQ], axis=0, keepdims=True)
    mean_d = jnp.mean(h[SEQ:], axis=0, keepdims=True)
    z = rms(h).astype(BF16)

    logits = mm(wr_ref[...], z, 1, 1)
    names = iota((NE, TOK), 0)
    here = (ids_ref[0:1, :] == names) | (ids_ref[1:2, :] == names)
    earlier = onehot(iota((TOK, TOK), 0) < iota((TOK, TOK), 1))
    rank = jnp.where(here, mm(onehot(here), earlier), -1.0)
    both_logits = jnp.sum(jnp.where(here, logits, 0.0), axis=0, keepdims=True)
    gate = jnp.where(here, 1.0 / (1.0 + jnp.exp(both_logits - 2.0 * logits)), 0.0)

    spread = onehot(iota((NE * MAIN, NE), 0) // MAIN == iota((NE * MAIN, NE), 1))
    slot = (iota((NE * MAIN, TOK), 0) % MAIN).astype(F32)
    main = mm(onehot(mm(spread, rank.astype(BF16)) == slot), z).astype(BF16)
    blocks[:, :, :D] = main.reshape(NE, MAIN, D)

    extra = mm(onehot(rank == float(MAIN)), z).astype(BF16)
    lane = iota((NE, 128), 1)
    gates_q = jnp.zeros((NE, 128), F32)
    gates_d = jnp.zeros((NE, 128), F32)
    for s in range(MAIN + 1):
        chosen = jnp.where(rank == float(s), gate, 0.0)
        gates_q = jnp.where(lane == s, jnp.sum(chosen[:, :SEQ], axis=1, keepdims=True), gates_q)
        gates_d = jnp.where(lane == s, jnp.sum(chosen[:, SEQ:], axis=1, keepdims=True), gates_d)
    parts = [extra[:, c * 128 : (c + 1) * 128] for c in range(D // 128)]
    stacked = jnp.concatenate(parts + [gates_q.astype(BF16), gates_d.astype(BF16)], axis=0)
    r, c = iota((NE * MAIN, 8 * NE), 0), iota((NE * MAIN, 8 * NE), 1)
    side = mm(onehot(c == (r % MAIN) * NE + r // MAIN), stacked).astype(BF16)
    blocks[:, :, D:] = side.reshape(NE, MAIN, 128)
    return mean_q, mean_d


def gelu_and_slope(x):
    a, b = 0.7978845608028654, 0.044715
    square = x * x
    t = jnp.tanh(a * x * (1.0 + b * square))
    half = 0.5 * (1.0 + t)
    slope = half + 0.5 * x * (1.0 - t * t) * (a * (1.0 + 3.0 * b * square))
    return (x * half).astype(BF16), slope.astype(BF16)


def pack_side(block):
    r, col = iota((SROWS, CROWS), 0), iota((SROWS, CROWS), 1)
    take = onehot(col == (r % SIZE) * MAIN + r // SIZE)
    return mm(take, block.reshape(CROWS, 128)).astype(BF16)


def expert_chunk(plane, c, rows, sides, up_ref, turned, extras, slopes, gates, acts):
    q = plane * CHUNKS + c
    main = rows[plane, pl.ds(c * SIZE, SIZE)].reshape(CROWS, ROW)[:, :D]
    turned[q] = main.T
    side = sides[q].astype(F32)
    extra = jnp.concatenate(
        [side[k * SIZE : (k + 1) * SIZE] for k in range(D // 128)], axis=1
    )
    extra = jnp.concatenate([extra, jnp.zeros((MAIN - SIZE, D), F32)]).astype(BF16)
    extras[q] = extra
    own = side[6 * SIZE :]
    wide = CROWS + 128
    s, j = iota((128, wide), 0), iota((128, wide), 1)
    repeat = onehot(s == jnp.where(j < CROWS, j % MAIN, MAIN))
    i, j = iota((2 * SIZE, wide), 0), iota((2 * SIZE, wide), 1)
    mine = jnp.where(j < CROWS, j // MAIN, j - CROWS) == i % SIZE
    gate = jnp.where(mine, mm(own.astype(BF16), repeat), 0.0).astype(BF16)
    gates[q] = gate[:, : CROWS + MAIN].T
    act, slope = gelu_and_slope(mm(main, up_ref[...]))
    act_x, slope_x = gelu_and_slope(mm(extra, up_ref[...]))
    slopes[q, :CROWS] = slope
    slopes[q, CROWS:] = slope_x
    total = mm(gate[:, :CROWS], act) + mm(gate[:, CROWS : CROWS + MAIN], act_x)
    acts[q] = total.astype(BF16)


def wide_of(i):
    return (i % (NE // 2)) * 2 + i // (NE // 2)


def sequence_order(w_here, transposed):
    n = 16 * NE
    a, b = (1, 0) if transposed else (0, 1)
    r, c = iota((n, n), a), iota((n, n), b)
    j = ((w_here + NE - wide_of(r // 16)) * UNSTRIDE) % NE
    row = ((r % 8) * CHUNKS + j // SIZE) * 16 + ((r // 8) % 2) * 8 + j % SIZE
    return onehot(c == row)


def split(v):
    high = v.astype(BF16)
    return high, (v - high.astype(F32)).astype(BF16)


def row_gradients(pooled, positive):
    pairs = 8 * NE
    query = pooled[:, :8].reshape(pairs, D)
    document = pooled[:, 8:].reshape(pairs, D)
    query_b, document_b = query.astype(BF16), document.astype(BF16)
    inverse_q = lax.rsqrt(jnp.sum(query * query, axis=-1, keepdims=True) + EPS)
    inverse_d = lax.rsqrt(jnp.sum(document * document, axis=-1, keepdims=True) + EPS)
    squares = mm(jnp.ones((8, D), F32), document * document, 1, 1, HIGHEST)
    inverse_row = lax.rsqrt(squares[0:1] + EPS)
    weights = jnp.exp(mm(query_b, document_b, 1, 1) * (inverse_q * WARMTH) * inverse_row)
    probs = weights / jnp.sum(weights, axis=1, keepdims=True)

    def number(j):
        return wide_of(j // 8) * 8 + j % 8

    r, c = iota((pairs, pairs), 0), iota((pairs, pairs), 1)
    target = mm(onehot(number(r) == c), onehot(number(r) == positive), 1, 1)
    excess = (probs - target) * (LOSS_SCALE * WARMTH)
    high, rest = split(excess * inverse_row)
    grad_q = mm(high, document_b) + mm(rest, document_b)
    high, rest = split(excess * inverse_q)
    grad_d = mm(high, query_b, 0, 0) + mm(rest, query_b, 0, 0)

    def back(row, grad, inverse):
        unit = row * inverse
        inner = jnp.sum(unit * grad, axis=-1, keepdims=True)
        return ((grad - unit * inner) * (inverse * (1.0 / SEQ))).reshape(NE, 8, D)

    both = [back(query, grad_q, inverse_q), back(document, grad_d, inverse_d)]
    return jnp.concatenate(both, axis=1).reshape(16 * NE, D).astype(BF16)


def each(start, stop, act):
    def one(i, carry):
        act(i)
        return carry

    lax.fori_loop(start, stop, one, 0)


def step_kernel(
    nw, nz,
    x_ref, ids_ref, positive_ref, wr_ref, wqkv_hbm, wout_hbm, up_hbm, down_hbm,
    grad_up_ref, grad_down_ref,
    wqkv_ref, wout_ref, up_ref, down_ref, load_sems,
    blocks, mixed, rows, sides, turned, extras, slopes, gates, acts, spread, dpre_x,
    ordered, part, lent, half, got, zsend, zgot, pooled,
    s1, r1, s2, r2, sem_core, s3, r3, s4, r4, s5, r5, s6, r6,
):
    w, z = lax.axis_index("wide"), lax.axis_index("narrow")
    right, left = lax.rem(z + 1, nz), lax.rem(z + nz - 1, nz)
    hops, chips = nz // 2, nw // 2
    chip, core = w // 2, lax.rem(w, 2)
    sibling = w + 1 - 2 * core

    class loads:
        steps = [
            [
                (
                    wqkv_hbm.at[:, pl.ds(third * D + block * 256, 256)],
                    wqkv_ref.at[:, pl.ds(third * D + block * 256, 256)],
                )
                for third in range(3)
            ]
            for block in range(D // 256)
        ] + [[(wout_hbm, wout_ref)], [(up_hbm, up_ref)], [(down_hbm, down_ref)]]

        def copies(step):
            return [
                pltpu.make_async_copy(source, target, load_sems.at[step, i])
                for i, (source, target) in enumerate(loads.steps[step])
            ]

        def start(step):
            for one in loads.copies(step):
                one.start()

        def wait(step):
            for one in loads.copies(step):
                one.wait()

    for step in range(len(loads.steps)):
        loads.start(step)

    barrier = pltpu.get_barrier_semaphore()

    def greet(peer):
        pl.semaphore_signal(barrier, inc=1, device_id=peer, device_id_type=MESH)

    each(1, nw, lambda d: greet((lax.rem(w + d, nw), z)))
    each(1, nz, lambda d: greet((w, lax.rem(z + d, nz))))

    mean_q, mean_d = front(
        loads, x_ref, ids_ref, wqkv_ref, wout_ref, wr_ref, blocks, mixed
    )
    for step in (-2, -1):
        loads.wait(len(loads.steps) + step)

    pl.semaphore_wait(barrier, nw + nz - 2)

    def copy(source, target, send, receive, peer):
        return pltpu.make_async_remote_copy(
            src_ref=source, dst_ref=target, send_sem=send, recv_sem=receive,
            device_id=peer, device_id_type=MESH,
        )

    def first(j):
        peer = lax.rem(w + STRIDE * j, nw)
        return copy(blocks.at[peer], rows.at[z, j], s1.at[j], r1.at[j], (peer, z))

    def send_chunk(c):
        each(jnp.maximum(c * SIZE, 1), (c + 1) * SIZE, lambda j: first(j).start())

    def arrived(c):
        def one(j):
            pltpu.make_async_copy(blocks.at[j], rows.at[z, j], r1.at[j]).wait()

        each(c * SIZE, (c + 1) * SIZE, one)

    class move:
        def __init__(self, way, hop, c):
            plane = lax.rem(z + nz + (2 * way - 1) * (hop - 1), nz)
            main = rows.at[plane, pl.ds(c * SIZE, SIZE), :, pl.ds(0, D)]
            self.copies = [
                copy(
                    block, block, s2.at[way, hop - 1, c, i], r2.at[way, hop - 1, c, i],
                    (w, right if way == 0 else left),
                )
                for i, block in enumerate((main, sides.at[plane * CHUNKS + c]))
            ]

        def start(self):
            for one in self.copies:
                one.start()

        def wait_recv(self):
            for one in self.copies:
                one.wait_recv()

        def wait_send(self):
            for one in self.copies:
                one.wait_send()

    def work(plane, c):
        expert_chunk(plane, c, rows, sides, up_ref, turned, extras, slopes, gates, acts)

    def work_both(hop, c):
        each(0, 2, lambda way: work(lax.rem(z + nz + (2 * way - 1) * hop, nz), c))

    pltpu.make_async_copy(blocks.at[w], rows.at[z, 0], r1.at[0]).start()
    for c in range(AHEAD):
        send_chunk(c)

    def home(c, more):
        arrived(c)
        sides[z * CHUNKS + c] = pack_side(rows[z, pl.ds(c * SIZE, SIZE), :, D:])
        for way in range(2):
            move(way, 1, c).start()
        if more:
            send_chunk(c + AHEAD)

    each(0, CHUNKS - AHEAD, lambda c: home(c, True))
    each(CHUNKS - AHEAD, CHUNKS, lambda c: home(c, False))

    def both_ways(hop, c, onward, behind):
        for way in range(2):
            move(way, hop, c).wait_recv()
            if way in onward:
                move(way, hop + 1, c).start()
        behind(c)

    each(0, CHUNKS, lambda c: both_ways(1, c, (0, 1), lambda c: work(z, c)))
    each(0, (hops - 3) * CHUNKS, lambda i: both_ways(
        2 + i // CHUNKS, lax.rem(i, CHUNKS), (0, 1), lambda c: work_both(1 + i // CHUNKS, c)
    ))
    half_way = CHUNKS // 2
    each(0, half_way, lambda c: both_ways(hops - 1, c, (0,), lambda c: work_both(hops - 2, c)))
    each(half_way, CHUNKS, lambda c: both_ways(hops - 1, c, (1,), lambda c: work_both(hops - 2, c)))
    each(0, CHUNKS, lambda c: work_both(hops - 1, c))

    def last(i):
        for way in range(2):
            move(way, hops, i + way * half_way).wait_recv()
        each(0, 2, lambda way: work(lax.rem(z + hops, nz), i + way * half_way))

    each(0, half_way, last)

    side = NE // 2 * 16
    ordered[...] = mm(sequence_order(w, False), acts[...].reshape(16 * NE, FB)).astype(BF16)

    def partial(which):
        return mm(ordered[pl.ds(pl.multiple_of(which * side, side), side)], down_ref[...])

    lent[...] = partial(1 - core).astype(BF16).reshape(lent.shape)
    swap = copy(lent, half, sem_core.at[0], sem_core.at[1], (sibling, z))
    swap.start()
    part[...] = partial(core).reshape(part.shape)
    swap.wait_recv()
    part[...] = part[...] + half[...].astype(F32)
    swap.wait_send()
    lent[...] = part[...].astype(BF16)

    def peer_chip(d):
        return lax.rem(chip + d, chips)

    def scatter(d):
        return copy(
            lent.at[peer_chip(d)], got.at[d], s3.at[d], r3.at[d], (peer_chip(d) * 2 + core, z)
        )

    def across(d):
        return copy(zsend, zgot.at[d], s4.at[d], r4.at[d], (w, lax.rem(z + d, nz)))

    def gather(d, origin):
        block = pooled.at[core, origin]
        return copy(block, block, s5.at[d], r5.at[d], (peer_chip(d) * 2 + core, z))

    def lend(d, origin, holder):
        block = pooled.at[holder, origin]
        return copy(block, block, s6.at[d], r6.at[d], (sibling, z))

    def summed(count, one_copy, buffer, start):
        def one(d, total):
            one_copy(d).wait_recv()
            return total + buffer[d].astype(F32)

        return lax.fori_loop(1, count, one, start)

    each(1, chips, lambda d: scatter(d).start())
    total = summed(chips, scatter, got, part[chip]) * (1.0 / SEQ)
    row = iota((16, 1), 0)
    total = total + jnp.where(row == z, mean_q, 0.0) + jnp.where(row == z + 8, mean_d, 0.0)
    zsend[...] = total.astype(BF16)
    each(1, nz, lambda d: across(d).start())
    pooled[core, chip] = summed(nz, across, zgot, total).astype(BF16)
    each(1, chips, lambda d: gather(d, chip).start())
    lend(0, chip, core).start()

    def pass_on(d):
        origin = lax.rem(chip - d + chips, chips)
        gather(d, origin).wait_recv()
        lend(d, origin, core).start()

    each(1, chips, pass_on)
    each(0, chips, lambda d: lend(d, lax.rem(chip - d + chips, chips), 1 - core).wait_recv())

    dy = row_gradients(pooled[...].reshape(NE, 16, D).astype(F32), positive_ref[...])
    grad_down_ref[...] = mm(ordered[...], dy, 0, 0)
    back = mm(dy, down_ref[...], 1, 1).astype(BF16)
    spread[...] = mm(sequence_order(w, True), back).astype(BF16).reshape(spread.shape)

    grad_up_ref[...] = jnp.zeros_like(grad_up_ref)

    def add(p):
        left_side, right_side = [], []
        for c in range(CHUNKS):
            q = p * CHUNKS + c
            product = mm(gates[q], spread[q]) * slopes[q].astype(F32)
            right_side.append(product[:CROWS].astype(BF16))
            dpre_x[q] = product[CROWS:].astype(BF16)
            left_side.append(turned[q])
        grad_up_ref[...] += mm(
            jnp.concatenate(left_side, axis=1), jnp.concatenate(right_side, axis=0)
        )

    each(0, nz, add)
    extra_rows = nz * CHUNKS * MAIN
    grad_up_ref[...] += mm(
        extras[...].reshape(extra_rows, D), dpre_x[...].reshape(extra_rows, FB), 0, 0
    )

    each(1, nw, lambda j: first(j).wait_send())
    for way in range(2):
        each(0, (hops - 1) * CHUNKS, lambda i: move(way, 1 + i // CHUNKS, lax.rem(i, CHUNKS)).wait_send())
        each(0, CHUNKS // 2, lambda i: move(way, hops, i + way * (CHUNKS // 2)).wait_send())
    each(1, chips, lambda d: scatter(d).wait_send())
    each(1, nz, lambda d: across(d).wait_send())
    each(1, chips, lambda d: gather(d, chip).wait_send())
    each(0, chips, lambda d: lend(d, lax.rem(chip - d + chips, chips), core).wait_send())


def body(pair_tokens, expert_ids, positive, w_qkv, w_out, w_router, w_up, w_down):
    nw, nz = lax.axis_size("wide"), lax.axis_size("narrow")
    chips, parts = nw // 2, nz * CHUNKS
    dma = pltpu.SemaphoreType.DMA
    vmem = pl.BlockSpec(memory_space=pltpu.VMEM)
    grad_up, grad_down = pl.pallas_call(
        functools.partial(step_kernel, nw, nz),
        out_shape=(
            jax.ShapeDtypeStruct((D, FB), F32),
            jax.ShapeDtypeStruct((FB, D), F32),
        ),
        in_specs=[vmem] * 4 + [pl.BlockSpec(memory_space=pl.ANY)] * 4,
        out_specs=(vmem, vmem),
        scratch_shapes=[
            pltpu.VMEM(w_qkv.shape, BF16),
            pltpu.VMEM(w_out.shape, BF16),
            pltpu.VMEM((D, FB), BF16),
            pltpu.VMEM((FB, D), BF16),
            dma((D // 256 + 3, 3)),
            pltpu.VMEM((NE, MAIN, ROW), BF16),
            pltpu.VMEM((TOK, D), BF16),
            pltpu.VMEM((nz, nw, MAIN, ROW), BF16),
            pltpu.VMEM((parts, SROWS, 128), BF16),
            pltpu.VMEM((parts, D, CROWS), BF16),
            pltpu.VMEM((parts, MAIN, D), BF16),
            pltpu.VMEM((parts, CROWS + MAIN, FB), BF16),
            pltpu.VMEM((parts, CROWS + MAIN, 2 * SIZE), BF16),
            pltpu.VMEM((parts, 2 * SIZE, FB), BF16),
            pltpu.VMEM((parts, 2 * SIZE, FB), BF16),
            pltpu.VMEM((parts, MAIN, FB), BF16),
            pltpu.VMEM((16 * NE, FB), BF16),
            pltpu.VMEM((chips, 16, D), F32),
            pltpu.VMEM((chips, 16, D), BF16),
            pltpu.VMEM((chips, 16, D), BF16),
            pltpu.VMEM((chips, 16, D), BF16),
            pltpu.VMEM((16, D), BF16),
            pltpu.VMEM((nz, 16, D), BF16),
            pltpu.VMEM((2, chips, 16, D), BF16),
            dma((nw,)), dma((nw,)),
            dma((2, nz // 2, CHUNKS, 2)), dma((2, nz // 2, CHUNKS, 2)),
            dma((2,)),
            dma((chips,)), dma((chips,)),
            dma((nz,)), dma((nz,)),
            dma((chips,)), dma((chips,)),
            dma((chips,)), dma((chips,)),
        ],
        compiler_params=pltpu.CompilerParams(
            collective_id=0, has_side_effects=True, vmem_limit_bytes=VMEM_BYTES
        ),
        name="contrastive_step",
    )(
        pair_tokens.reshape(TOK, D),
        expert_ids.reshape(TOK, 2).T,
        positive.reshape(1, -1),
        w_router.T,
        w_qkv,
        w_out,
        w_up[0],
        w_down[0],
    )
    return (grad_up[None], grad_down[None])


def solution(mesh):
    return jax.shard_map(
        body,
        mesh=mesh,
        in_specs=(
            P(("wide", "narrow"), None, None, None),
            P(("wide", "narrow"), None, None),
            P(),
            P(),
            P(),
            P(),
            P("wide", None, "narrow"),
            P("wide", "narrow", None),
        ),
        out_specs=(P("wide", None, "narrow"), P("wide", "narrow", None)),
        check_vma=False,
    )
```

```python
import functools

import jax
import jax.numpy as jnp
from jax import lax
from jax.experimental import pallas as pl
from jax.experimental.pallas import tpu as pltpu
from jax.sharding import PartitionSpec as P

D = 768
FB = 384
SEQ = 128
TOK = 256
NE = 32
MAIN = 16
ROW = D + 128
CHUNKS = 4
SIZE = NE // CHUNKS
CROWS = SIZE * MAIN
SROWS = SIZE * 8
STRIDE, UNSTRIDE = 11, 3
EPS = 1e-06
WARMTH = 20.0
LOSS_SCALE = 64.0
VMEM_BYTES = 56 * 2**20
MESH = pl.DeviceIdType.MESH
HIGHEST = lax.Precision.HIGHEST
F32, BF16, I32 = jnp.float32, jnp.bfloat16, jnp.int32


def mm(a, b, ca=1, cb=0, precision=None):
    return lax.dot_general(
        a, b, (((ca,), (cb,)), ((), ())), precision=precision, preferred_element_type=F32
    )


def iota(shape, axis):
    return lax.broadcasted_iota(I32, shape, axis)


def onehot(condition):
    return jnp.where(condition, 1.0, 0.0).astype(BF16)


def rms(v):
    return v * lax.rsqrt(jnp.mean(v * v, axis=-1, keepdims=True) + EPS)


def front(loads, x_ref, ids_ref, wqkv_ref, wout_ref, wr_ref, blocks, mixed):
    normed = rms(x_ref[...].astype(F32)).astype(BF16)
    wide = 256
    same_head = onehot(iota((wide, wide), 0) // 64 == iota((wide, wide), 1) // 64)
    low = iota((SEQ, 128), 1) < 64
    ones = jnp.ones((SEQ, 128), BF16)

    def head_rms(v):
        square = v * v
        high = square.astype(BF16)
        rest = (square - high.astype(F32)).astype(BF16)
        mean = (mm(high, same_head) + mm(rest, same_head)) * (1.0 / 64.0)
        return (v * lax.rsqrt(mean + EPS)).astype(BF16)

    for block in range(D // wide):
        at = block * wide
        loads.wait(block)
        q = head_rms(mm(normed, wqkv_ref[:, at : at + wide]))
        k = head_rms(mm(normed, wqkv_ref[:, D + at : D + at + wide]))
        v = mm(normed, wqkv_ref[:, 2 * D + at : 2 * D + at + wide]).astype(BF16)
        for s in range(TOK // SEQ):
            rows = slice(s * SEQ, (s + 1) * SEQ)
            for c in range(wide // 128):
                lanes = slice(c * 128, (c + 1) * 128)
                qc, kc = q[rows, lanes], k[rows, lanes]
                values = jnp.concatenate([v[rows, lanes], ones], axis=1)
                heads = []
                for half in range(2):
                    qh = jnp.where(low if half == 0 else ~low, qc, jnp.zeros_like(qc))
                    weights = jnp.exp(mm(qh, kc, 1, 1) * 0.125).astype(BF16)
                    both = mm(weights, values)
                    heads.append(both[:, :128] / both[:, 128:])
                mixed[rows, at + c * 128 : at + (c + 1) * 128] = jnp.where(
                    low, heads[0], heads[1]
                ).astype(BF16)

    loads.wait(D // wide)
    h = (x_ref[...].astype(F32) + mm(mixed[...], wout_ref[...])).astype(BF16).astype(F32)
    mean_q = jnp.mean(h[:SEQ], axis=0, keepdims=True)
    mean_d = jnp.mean(h[SEQ:], axis=0, keepdims=True)
    z = rms(h).astype(BF16)

    logits = mm(wr_ref[...], z, 1, 1)
    names = iota((NE, TOK), 0)
    here = (ids_ref[0:1, :] == names) | (ids_ref[1:2, :] == names)
    earlier = onehot(iota((TOK, TOK), 0) < iota((TOK, TOK), 1))
    rank = jnp.where(here, mm(onehot(here), earlier), -1.0)
    both_logits = jnp.sum(jnp.where(here, logits, 0.0), axis=0, keepdims=True)
    gate = jnp.where(here, 1.0 / (1.0 + jnp.exp(both_logits - 2.0 * logits)), 0.0)

    spread = onehot(iota((NE * MAIN, NE), 0) // MAIN == iota((NE * MAIN, NE), 1))
    slot = (iota((NE * MAIN, TOK), 0) % MAIN).astype(F32)
    main = mm(onehot(mm(spread, rank.astype(BF16)) == slot), z).astype(BF16)
    blocks[:, :, :D] = main.reshape(NE, MAIN, D)

    extra = mm(onehot(rank == float(MAIN)), z).astype(BF16)
    lane = iota((NE, 128), 1)
    gates_q = jnp.zeros((NE, 128), F32)
    gates_d = jnp.zeros((NE, 128), F32)
    for s in range(MAIN + 1):
        chosen = jnp.where(rank == float(s), gate, 0.0)
        gates_q = jnp.where(lane == s, jnp.sum(chosen[:, :SEQ], axis=1, keepdims=True), gates_q)
        gates_d = jnp.where(lane == s, jnp.sum(chosen[:, SEQ:], axis=1, keepdims=True), gates_d)
    parts = [extra[:, c * 128 : (c + 1) * 128] for c in range(D // 128)]
    stacked = jnp.concatenate(parts + [gates_q.astype(BF16), gates_d.astype(BF16)], axis=0)
    r, c = iota((NE * MAIN, 8 * NE), 0), iota((NE * MAIN, 8 * NE), 1)
    side = mm(onehot(c == (r % MAIN) * NE + r // MAIN), stacked).astype(BF16)
    blocks[:, :, D:] = side.reshape(NE, MAIN, 128)
    return mean_q, mean_d


def gelu_and_slope(x):
    a, b = 0.7978845608028654, 0.044715
    square = x * x
    t = jnp.tanh(a * x * (1.0 + b * square))
    half = 0.5 * (1.0 + t)
    slope = half + 0.5 * x * (1.0 - t * t) * (a * (1.0 + 3.0 * b * square))
    return (x * half).astype(BF16), slope.astype(BF16)


def pack_side(block):
    r, col = iota((SROWS, CROWS), 0), iota((SROWS, CROWS), 1)
    take = onehot(col == (r % SIZE) * MAIN + r // SIZE)
    return mm(take, block.reshape(CROWS, 128)).astype(BF16)


def expert_chunk(plane, c, rows, sides, up_ref, turned, extras, slopes, gates, acts):
    q = plane * CHUNKS + c
    main = rows[plane, pl.ds(c * SIZE, SIZE)].reshape(CROWS, ROW)[:, :D]
    turned[q] = main.T
    side = sides[q].astype(F32)
    extra = jnp.concatenate(
        [side[k * SIZE : (k + 1) * SIZE] for k in range(D // 128)], axis=1
    )
    extra = jnp.concatenate([extra, jnp.zeros((MAIN - SIZE, D), F32)]).astype(BF16)
    extras[q] = extra
    own = side[6 * SIZE :]
    wide = CROWS + 128
    s, j = iota((128, wide), 0), iota((128, wide), 1)
    repeat = onehot(s == jnp.where(j < CROWS, j % MAIN, MAIN))
    i, j = iota((2 * SIZE, wide), 0), iota((2 * SIZE, wide), 1)
    mine = jnp.where(j < CROWS, j // MAIN, j - CROWS) == i % SIZE
    gate = jnp.where(mine, mm(own.astype(BF16), repeat), 0.0).astype(BF16)
    gates[q] = gate[:, : CROWS + MAIN].T
    act, slope = gelu_and_slope(mm(main, up_ref[...]))
    act_x, slope_x = gelu_and_slope(mm(extra, up_ref[...]))
    slopes[q, :CROWS] = slope
    slopes[q, CROWS:] = slope_x
    total = mm(gate[:, :CROWS], act) + mm(gate[:, CROWS : CROWS + MAIN], act_x)
    acts[q] = total.astype(BF16)


def wide_of(i):
    return (i % (NE // 2)) * 2 + i // (NE // 2)


def sequence_order(w_here, transposed):
    n = 16 * NE
    a, b = (1, 0) if transposed else (0, 1)
    r, c = iota((n, n), a), iota((n, n), b)
    j = ((w_here + NE - wide_of(r // 16)) * UNSTRIDE) % NE
    row = ((r % 8) * CHUNKS + j // SIZE) * 16 + ((r // 8) % 2) * 8 + j % SIZE
    return onehot(c == row)


def late_rows(w_here, acts, down):
    pieces, count = D // 128, CHUNKS * 2 * SIZE
    part = mm(acts.reshape(count, FB), down).astype(BF16)
    stacked = jnp.concatenate([part[:, k * 128 : (k + 1) * 128] for k in range(pieces)], axis=0)
    r, c = iota((NE * 16, pieces * count), 0), iota((NE * 16, pieces * count), 1)
    j = ((w_here + NE - wide_of(r // 16)) * UNSTRIDE) % NE
    kind, piece = (r % 16) // pieces, (r % 16) % pieces
    source = piece * count + (j // SIZE) * (2 * SIZE) + kind * SIZE + j % SIZE
    return mm(onehot((c == source) & (kind < 2)), stacked).reshape(2, NE // 2, 16, 128)


def split(v):
    high = v.astype(BF16)
    return high, (v - high.astype(F32)).astype(BF16)


def row_gradients(pooled, positive):
    pairs = 8 * NE
    query = pooled[:, :8].reshape(pairs, D)
    document = pooled[:, 8:].reshape(pairs, D)
    query_b, document_b = query.astype(BF16), document.astype(BF16)
    inverse_q = lax.rsqrt(jnp.sum(query * query, axis=-1, keepdims=True) + EPS)
    inverse_d = lax.rsqrt(jnp.sum(document * document, axis=-1, keepdims=True) + EPS)
    squares = mm(jnp.ones((8, D), F32), document * document, 1, 1, HIGHEST)
    inverse_row = lax.rsqrt(squares[0:1] + EPS)
    weights = jnp.exp(mm(query_b, document_b, 1, 1) * (inverse_q * WARMTH) * inverse_row)
    probs = weights / jnp.sum(weights, axis=1, keepdims=True)

    def number(j):
        return wide_of(j // 8) * 8 + j % 8

    r, c = iota((pairs, pairs), 0), iota((pairs, pairs), 1)
    target = mm(onehot(number(r) == c), onehot(number(r) == positive), 1, 1)
    excess = (probs - target) * (LOSS_SCALE * WARMTH)
    high, rest = split(excess * inverse_row)
    grad_q = mm(high, document_b) + mm(rest, document_b)
    high, rest = split(excess * inverse_q)
    grad_d = mm(high, query_b, 0, 0) + mm(rest, query_b, 0, 0)

    def back(row, grad, inverse):
        unit = row * inverse
        inner = jnp.sum(unit * grad, axis=-1, keepdims=True)
        return ((grad - unit * inner) * (inverse * (1.0 / SEQ))).reshape(NE, 8, D)

    both = [back(query, grad_q, inverse_q), back(document, grad_d, inverse_d)]
    return jnp.concatenate(both, axis=1).reshape(16 * NE, D).astype(BF16)


def each(start, stop, act):
    def one(i, carry):
        act(i)
        return carry

    lax.fori_loop(start, stop, one, 0)


def step_kernel(
    nw, nz,
    x_ref, ids_ref, positive_ref, wr_ref, wqkv_hbm, wout_hbm, up_hbm, down_hbm,
    grad_up_ref, grad_down_ref,
    wqkv_ref, wout_ref, up_ref, down_ref, load_sems,
    blocks, mixed, rows, sides, turned, extras, slopes, gates, acts, spread, dpre_x,
    ordered, part, lent, half, got, late_all, late_lent, late_half, late_send, late_got, zsend, zgot, pooled,
    s1, r1, s2, r2, sem_core, s3, r3, s4, r4, s5, r5, s6, r6, s7, r7,
):
    w, z = lax.axis_index("wide"), lax.axis_index("narrow")
    right, left = lax.rem(z + 1, nz), lax.rem(z + nz - 1, nz)
    hops, chips = nz // 2, nw // 2
    chip, core = w // 2, lax.rem(w, 2)
    sibling = w + 1 - 2 * core

    class loads:
        steps = [
            [
                (
                    wqkv_hbm.at[:, pl.ds(third * D + block * 256, 256)],
                    wqkv_ref.at[:, pl.ds(third * D + block * 256, 256)],
                )
                for third in range(3)
            ]
            for block in range(D // 256)
        ] + [[(wout_hbm, wout_ref)], [(up_hbm, up_ref)], [(down_hbm, down_ref)]]

        def copies(step):
            return [
                pltpu.make_async_copy(source, target, load_sems.at[step, i])
                for i, (source, target) in enumerate(loads.steps[step])
            ]

        def start(step):
            for one in loads.copies(step):
                one.start()

        def wait(step):
            for one in loads.copies(step):
                one.wait()

    for step in range(len(loads.steps)):
        loads.start(step)

    barrier = pltpu.get_barrier_semaphore()

    def greet(peer):
        pl.semaphore_signal(barrier, inc=1, device_id=peer, device_id_type=MESH)

    each(1, nw, lambda d: greet((lax.rem(w + d, nw), z)))
    each(1, nz, lambda d: greet((w, lax.rem(z + d, nz))))

    mean_q, mean_d = front(
        loads, x_ref, ids_ref, wqkv_ref, wout_ref, wr_ref, blocks, mixed
    )
    for step in (-2, -1):
        loads.wait(len(loads.steps) + step)

    pl.semaphore_wait(barrier, nw + nz - 2)

    def copy(source, target, send, receive, peer):
        return pltpu.make_async_remote_copy(
            src_ref=source, dst_ref=target, send_sem=send, recv_sem=receive,
            device_id=peer, device_id_type=MESH,
        )

    def first(j):
        peer = lax.rem(w + STRIDE * j, nw)
        return copy(blocks.at[peer], rows.at[z, j], s1.at[j], r1.at[j], (peer, z))

    def send_chunk(c):
        each(jnp.maximum(c * SIZE, 1), (c + 1) * SIZE, lambda j: first(j).start())

    def onward(way, j):
        block = rows.at[z, j, :, pl.ds(0, D)]
        c = j // SIZE
        return copy(
            block, block, s2.at[way, 0, c, 0], r2.at[way, 0, c, 0],
            (w, right if way == 0 else left),
        )

    def arrived(c):
        def one(j):
            pltpu.make_async_copy(blocks.at[j], rows.at[z, j], r1.at[j]).wait()
            for way in range(2):
                onward(way, j).start()

        each(c * SIZE, (c + 1) * SIZE, one)

    class move:
        def __init__(self, way, hop, c, items=(0, 1)):
            plane = lax.rem(z + nz + (2 * way - 1) * (hop - 1), nz)
            main = rows.at[plane, pl.ds(c * SIZE, SIZE), :, pl.ds(0, D)]
            blocks = (main, sides.at[plane * CHUNKS + c])
            self.copies = [
                copy(
                    blocks[i], blocks[i], s2.at[way, hop - 1, c, i], r2.at[way, hop - 1, c, i],
                    (w, right if way == 0 else left),
                )
                for i in items
            ]

        def start(self):
            for one in self.copies:
                one.start()

        def wait_recv(self):
            for one in self.copies:
                one.wait_recv()

        def wait_send(self):
            for one in self.copies:
                one.wait_send()

    def work(plane, c):
        expert_chunk(plane, c, rows, sides, up_ref, turned, extras, slopes, gates, acts)

    def work_both(hop, c):
        each(0, 2, lambda way: work(lax.rem(z + nz + (2 * way - 1) * hop, nz), c))

    pltpu.make_async_copy(blocks.at[w], rows.at[z, 0], r1.at[0]).start()
    each(0, CHUNKS, send_chunk)

    def home(c):
        arrived(c)
        sides[z * CHUNKS + c] = pack_side(rows[z, pl.ds(c * SIZE, SIZE), :, D:])
        for way in range(2):
            move(way, 1, c, (1,)).start()

    each(0, CHUNKS, home)

    def both_ways(hop, c, onward, behind):
        for way in range(2):
            move(way, hop, c).wait_recv()
            if way in onward:
                move(way, hop + 1, c).start()
        behind(c)

    each(0, CHUNKS, lambda c: both_ways(1, c, (0, 1), lambda c: work(z, c)))
    each(0, (hops - 3) * CHUNKS, lambda i: both_ways(
        2 + i // CHUNKS, lax.rem(i, CHUNKS), (0, 1), lambda c: work_both(1 + i // CHUNKS, c)
    ))
    half_way = CHUNKS // 2
    each(0, half_way, lambda c: both_ways(hops - 1, c, (0,), lambda c: work_both(hops - 2, c)))
    each(half_way, CHUNKS, lambda c: both_ways(hops - 1, c, (1,), lambda c: work_both(hops - 2, c)))
    each(0, CHUNKS, lambda c: work_both(hops - 1, c))

    far = lax.rem(z + hops, nz)
    acts[pl.ds(far * CHUNKS, CHUNKS)] = jnp.zeros((CHUNKS, 2 * SIZE, FB), BF16)
    side = NE // 2 * 16
    ordered[...] = mm(sequence_order(w, False), acts[...].reshape(16 * NE, FB)).astype(BF16)

    def partial(which):
        return mm(ordered[pl.ds(pl.multiple_of(which * side, side), side)], down_ref[...])

    lent[...] = partial(1 - core).astype(BF16).reshape(lent.shape)
    swap = copy(lent, half, sem_core.at[0], sem_core.at[1], (sibling, z))
    swap.start()
    part[...] = partial(core).reshape(part.shape)
    swap.wait_recv()
    part[...] = part[...] + half[...].astype(F32)
    swap.wait_send()
    lent[...] = part[...].astype(BF16)

    def peer_chip(d):
        return lax.rem(chip + d, chips)

    def scatter(d):
        return copy(
            lent.at[peer_chip(d)], got.at[d], s3.at[d], r3.at[d], (peer_chip(d) * 2 + core, z)
        )

    def across(d):
        return copy(zsend, zgot.at[d], s4.at[d], r4.at[d], (w, lax.rem(z + d, nz)))

    def gather(d, origin):
        block = pooled.at[core, origin]
        return copy(block, block, s5.at[d], r5.at[d], (peer_chip(d) * 2 + core, z))

    def lend(d, origin, holder):
        block = pooled.at[holder, origin]
        return copy(block, block, s6.at[d], r6.at[d], (sibling, z))

    each(1, chips, lambda d: scatter(d).start())

    def last(i):
        for way in range(2):
            move(way, hops, i + way * half_way).wait_recv()
        each(0, 2, lambda way: work(lax.rem(z + hops, nz), i + way * half_way))

    each(0, half_way, last)

    def summed(count, one_copy, buffer, start):
        def one(d, total):
            one_copy(d).wait_recv()
            return total + buffer[d].astype(F32)

        return lax.fori_loop(1, count, one, start)

    late_all[...] = late_rows(w, acts[pl.ds(far * CHUNKS, CHUNKS)], down_ref[...])
    late_lent[...] = late_all[1 - core].astype(BF16)
    late_swap = copy(late_lent, late_half, sem_core.at[2], sem_core.at[3], (sibling, z))
    late_swap.start()
    late_swap.wait_recv()
    late_part = late_all[core] + late_half[...].astype(F32)
    late_all[core] = late_part
    late_send[...] = late_part.astype(BF16)

    def late_scatter(d):
        return copy(
            late_send.at[peer_chip(d)], late_got.at[d], s7.at[d], r7.at[d],
            (peer_chip(d) * 2 + core, z),
        )

    each(1, chips, lambda d: late_scatter(d).start())
    total = summed(chips, scatter, got, part[chip])
    late = summed(chips, late_scatter, late_got, late_all[core, chip])
    row = iota((16, 1), 0)
    pieces = D // 128
    total = total + jnp.concatenate(
        [
            jnp.where(row == far, late[k : k + 1], 0.0)
            + jnp.where(row == far + 8, late[pieces + k : pieces + k + 1], 0.0)
            for k in range(pieces)
        ],
        axis=1,
    )
    total = total * (1.0 / SEQ)
    total = total + jnp.where(row == z, mean_q, 0.0) + jnp.where(row == z + 8, mean_d, 0.0)
    zsend[...] = total.astype(BF16)
    each(1, nz, lambda d: across(d).start())
    ordered[...] = mm(sequence_order(w, False), acts[...].reshape(16 * NE, FB)).astype(BF16)
    pooled[core, chip] = summed(nz, across, zgot, total).astype(BF16)
    each(1, chips, lambda d: gather(d, chip).start())
    lend(0, chip, core).start()

    def pass_on(d):
        origin = lax.rem(chip - d + chips, chips)
        gather(d, origin).wait_recv()
        lend(d, origin, core).start()

    each(1, chips, pass_on)
    each(0, chips, lambda d: lend(d, lax.rem(chip - d + chips, chips), 1 - core).wait_recv())

    dy = row_gradients(pooled[...].reshape(NE, 16, D).astype(F32), positive_ref[...])
    grad_down_ref[...] = mm(ordered[...], dy, 0, 0)
    back = mm(dy, down_ref[...], 1, 1).astype(BF16)
    spread[...] = mm(sequence_order(w, True), back).astype(BF16).reshape(spread.shape)

    grad_up_ref[...] = jnp.zeros_like(grad_up_ref)

    def add(p):
        left_side, right_side = [], []
        for c in range(CHUNKS):
            q = p * CHUNKS + c
            product = mm(gates[q], spread[q]) * slopes[q].astype(F32)
            right_side.append(product[:CROWS].astype(BF16))
            dpre_x[q] = product[CROWS:].astype(BF16)
            left_side.append(turned[q])
        grad_up_ref[...] += mm(
            jnp.concatenate(left_side, axis=1), jnp.concatenate(right_side, axis=0)
        )

    each(0, nz, add)
    extra_rows = nz * CHUNKS * MAIN
    grad_up_ref[...] += mm(
        extras[...].reshape(extra_rows, D), dpre_x[...].reshape(extra_rows, FB), 0, 0
    )

    each(1, nw, lambda j: first(j).wait_send())
    for way in range(2):
        each(0, (hops - 1) * CHUNKS, lambda i: move(way, 1 + i // CHUNKS, lax.rem(i, CHUNKS)).wait_send())
        each(0, CHUNKS // 2, lambda i: move(way, hops, i + way * (CHUNKS // 2)).wait_send())
    each(1, chips, lambda d: scatter(d).wait_send())
    late_swap.wait_send()
    each(1, chips, lambda d: late_scatter(d).wait_send())
    each(1, nz, lambda d: across(d).wait_send())
    each(1, chips, lambda d: gather(d, chip).wait_send())
    each(0, chips, lambda d: lend(d, lax.rem(chip - d + chips, chips), core).wait_send())


def body(pair_tokens, expert_ids, positive, w_qkv, w_out, w_router, w_up, w_down):
    nw, nz = lax.axis_size("wide"), lax.axis_size("narrow")
    chips, parts = nw // 2, nz * CHUNKS
    dma = pltpu.SemaphoreType.DMA
    vmem = pl.BlockSpec(memory_space=pltpu.VMEM)
    grad_up, grad_down = pl.pallas_call(
        functools.partial(step_kernel, nw, nz),
        out_shape=(
            jax.ShapeDtypeStruct((D, FB), F32),
            jax.ShapeDtypeStruct((FB, D), F32),
        ),
        in_specs=[vmem] * 4 + [pl.BlockSpec(memory_space=pl.ANY)] * 4,
        out_specs=(vmem, vmem),
        scratch_shapes=[
            pltpu.VMEM(w_qkv.shape, BF16),
            pltpu.VMEM(w_out.shape, BF16),
            pltpu.VMEM((D, FB), BF16),
            pltpu.VMEM((FB, D), BF16),
            dma((D // 256 + 3, 3)),
            pltpu.VMEM((NE, MAIN, ROW), BF16),
            pltpu.VMEM((TOK, D), BF16),
            pltpu.VMEM((nz, nw, MAIN, ROW), BF16),
            pltpu.VMEM((parts, SROWS, 128), BF16),
            pltpu.VMEM((parts, D, CROWS), BF16),
            pltpu.VMEM((parts, MAIN, D), BF16),
            pltpu.VMEM((parts, CROWS + MAIN, FB), BF16),
            pltpu.VMEM((parts, CROWS + MAIN, 2 * SIZE), BF16),
            pltpu.VMEM((parts, 2 * SIZE, FB), BF16),
            pltpu.VMEM((parts, 2 * SIZE, FB), BF16),
            pltpu.VMEM((parts, MAIN, FB), BF16),
            pltpu.VMEM((16 * NE, FB), BF16),
            pltpu.VMEM((chips, 16, D), F32),
            pltpu.VMEM((chips, 16, D), BF16),
            pltpu.VMEM((chips, 16, D), BF16),
            pltpu.VMEM((chips, 16, D), BF16),
            pltpu.VMEM((2, chips, 16, 128), F32),
            pltpu.VMEM((chips, 16, 128), BF16),
            pltpu.VMEM((chips, 16, 128), BF16),
            pltpu.VMEM((chips, 16, 128), BF16),
            pltpu.VMEM((chips, 16, 128), BF16),
            pltpu.VMEM((16, D), BF16),
            pltpu.VMEM((nz, 16, D), BF16),
            pltpu.VMEM((2, chips, 16, D), BF16),
            dma((nw,)), dma((nw,)),
            dma((2, nz // 2, CHUNKS, 2)), dma((2, nz // 2, CHUNKS, 2)),
            dma((4,)),
            dma((chips,)), dma((chips,)),
            dma((nz,)), dma((nz,)),
            dma((chips,)), dma((chips,)),
            dma((chips,)), dma((chips,)),
            dma((chips,)), dma((chips,)),
        ],
        compiler_params=pltpu.CompilerParams(
            collective_id=0, has_side_effects=True, vmem_limit_bytes=VMEM_BYTES
        ),
        name="contrastive_step",
    )(
        pair_tokens.reshape(TOK, D),
        expert_ids.reshape(TOK, 2).T,
        positive.reshape(1, -1),
        w_router.T,
        w_qkv,
        w_out,
        w_up[0],
        w_down[0],
    )
    return (grad_up[None], grad_down[None])


def solution(mesh):
    return jax.shard_map(
        body,
        mesh=mesh,
        in_specs=(
            P(("wide", "narrow"), None, None, None),
            P(("wide", "narrow"), None, None),
            P(),
            P(),
            P(),
            P(),
            P("wide", None, "narrow"),
            P("wide", "narrow", None),
        ),
        out_specs=(P("wide", None, "narrow"), P("wide", "narrow", None)),
        check_vma=False,
    )
```

```python
import functools

import jax
import jax.numpy as jnp
from jax import lax
from jax.experimental import pallas as pl
from jax.experimental.pallas import tpu as pltpu
from jax.sharding import PartitionSpec as P

D = 768
FB = 384
SEQ = 128
TOK = 256
NE = 32
MAIN = 16
ROW = D + 128
CHUNKS = 4
SIZE = NE // CHUNKS
CROWS = SIZE * MAIN
SROWS = SIZE * 8
STRIDE, UNSTRIDE = 11, 3
EPS = 1e-06
WARMTH = 20.0
LOSS_SCALE = 64.0
VMEM_BYTES = 56 * 2**20
MESH = pl.DeviceIdType.MESH
HIGHEST = lax.Precision.HIGHEST
F32, BF16, I32 = jnp.float32, jnp.bfloat16, jnp.int32


def mm(a, b, ca=1, cb=0, precision=None):
    return lax.dot_general(
        a, b, (((ca,), (cb,)), ((), ())), precision=precision, preferred_element_type=F32
    )


def iota(shape, axis):
    return lax.broadcasted_iota(I32, shape, axis)


def onehot(condition):
    return jnp.where(condition, 1.0, 0.0).astype(BF16)


def rms(v):
    return v * lax.rsqrt(jnp.mean(v * v, axis=-1, keepdims=True) + EPS)


def front(loads, x_ref, ids_ref, wqkv_ref, wout_ref, wr_ref, blocks, mixed):
    normed = rms(x_ref[...].astype(F32)).astype(BF16)
    wide = 256
    same_head = onehot(iota((wide, wide), 0) // 64 == iota((wide, wide), 1) // 64)
    low = iota((SEQ, 128), 1) < 64
    ones = jnp.ones((SEQ, 128), BF16)

    def head_rms(v):
        square = v * v
        high = square.astype(BF16)
        rest = (square - high.astype(F32)).astype(BF16)
        mean = (mm(high, same_head) + mm(rest, same_head)) * (1.0 / 64.0)
        return (v * lax.rsqrt(mean + EPS)).astype(BF16)

    for block in range(D // wide):
        at = block * wide
        loads.wait(block)
        q = head_rms(mm(normed, wqkv_ref[:, at : at + wide]))
        k = head_rms(mm(normed, wqkv_ref[:, D + at : D + at + wide]))
        v = mm(normed, wqkv_ref[:, 2 * D + at : 2 * D + at + wide]).astype(BF16)
        for s in range(TOK // SEQ):
            rows = slice(s * SEQ, (s + 1) * SEQ)
            for c in range(wide // 128):
                lanes = slice(c * 128, (c + 1) * 128)
                qc, kc = q[rows, lanes], k[rows, lanes]
                values = jnp.concatenate([v[rows, lanes], ones], axis=1)
                heads = []
                for half in range(2):
                    qh = jnp.where(low if half == 0 else ~low, qc, jnp.zeros_like(qc))
                    weights = jnp.exp(mm(qh, kc, 1, 1) * 0.125).astype(BF16)
                    both = mm(weights, values)
                    heads.append(both[:, :128] / both[:, 128:])
                mixed[rows, at + c * 128 : at + (c + 1) * 128] = jnp.where(
                    low, heads[0], heads[1]
                ).astype(BF16)

    loads.wait(D // wide)
    h = (x_ref[...].astype(F32) + mm(mixed[...], wout_ref[...])).astype(BF16).astype(F32)
    mean_q = jnp.mean(h[:SEQ], axis=0, keepdims=True)
    mean_d = jnp.mean(h[SEQ:], axis=0, keepdims=True)
    z = rms(h).astype(BF16)

    logits = mm(wr_ref[...], z, 1, 1)
    names = iota((NE, TOK), 0)
    here = (ids_ref[0:1, :] == names) | (ids_ref[1:2, :] == names)
    earlier = onehot(iota((TOK, TOK), 0) < iota((TOK, TOK), 1))
    rank = jnp.where(here, mm(onehot(here), earlier), -1.0)
    both_logits = jnp.sum(jnp.where(here, logits, 0.0), axis=0, keepdims=True)
    gate = jnp.where(here, 1.0 / (1.0 + jnp.exp(both_logits - 2.0 * logits)), 0.0)

    spread = onehot(iota((NE * MAIN, NE), 0) // MAIN == iota((NE * MAIN, NE), 1))
    slot = (iota((NE * MAIN, TOK), 0) % MAIN).astype(F32)
    main = mm(onehot(mm(spread, rank.astype(BF16)) == slot), z).astype(BF16)
    blocks[:, :, :D] = main.reshape(NE, MAIN, D)

    extra = mm(onehot(rank == float(MAIN)), z).astype(BF16)
    lane = iota((NE, 128), 1)
    gates_q = jnp.zeros((NE, 128), F32)
    gates_d = jnp.zeros((NE, 128), F32)
    for s in range(MAIN + 1):
        chosen = jnp.where(rank == float(s), gate, 0.0)
        gates_q = jnp.where(lane == s, jnp.sum(chosen[:, :SEQ], axis=1, keepdims=True), gates_q)
        gates_d = jnp.where(lane == s, jnp.sum(chosen[:, SEQ:], axis=1, keepdims=True), gates_d)
    parts = [extra[:, c * 128 : (c + 1) * 128] for c in range(D // 128)]
    stacked = jnp.concatenate(parts + [gates_q.astype(BF16), gates_d.astype(BF16)], axis=0)
    r, c = iota((NE * MAIN, 8 * NE), 0), iota((NE * MAIN, 8 * NE), 1)
    side = mm(onehot(c == (r % MAIN) * NE + r // MAIN), stacked).astype(BF16)
    blocks[:, :, D:] = side.reshape(NE, MAIN, 128)
    return mean_q, mean_d


def gelu_and_slope(x):
    a, b = 0.7978845608028654, 0.044715
    square = x * x
    t = jnp.tanh(a * x * (1.0 + b * square))
    half = 0.5 * (1.0 + t)
    slope = half + 0.5 * x * (1.0 - t * t) * (a * (1.0 + 3.0 * b * square))
    return (x * half).astype(BF16), slope.astype(BF16)


def pack_side(block):
    r, col = iota((SROWS, CROWS), 0), iota((SROWS, CROWS), 1)
    take = onehot(col == (r % SIZE) * MAIN + r // SIZE)
    return mm(take, block.reshape(CROWS, 128)).astype(BF16)


def expert_chunk(plane, c, rows, sides, up_ref, turned, extras, slopes, gates, acts):
    q = plane * CHUNKS + c
    main = rows[plane, pl.ds(c * SIZE, SIZE)].reshape(CROWS, ROW)[:, :D]
    turned[q] = main.T
    side = sides[q].astype(F32)
    extra = jnp.concatenate(
        [side[k * SIZE : (k + 1) * SIZE] for k in range(D // 128)], axis=1
    )
    extra = jnp.concatenate([extra, jnp.zeros((MAIN - SIZE, D), F32)]).astype(BF16)
    extras[q] = extra
    own = side[6 * SIZE :]
    wide = CROWS + 128
    s, j = iota((128, wide), 0), iota((128, wide), 1)
    repeat = onehot(s == jnp.where(j < CROWS, j % MAIN, MAIN))
    i, j = iota((2 * SIZE, wide), 0), iota((2 * SIZE, wide), 1)
    mine = jnp.where(j < CROWS, j // MAIN, j - CROWS) == i % SIZE
    gate = jnp.where(mine, mm(own.astype(BF16), repeat), 0.0).astype(BF16)
    gates[q] = gate[:, : CROWS + MAIN].T
    act, slope = gelu_and_slope(mm(main, up_ref[...]))
    act_x, slope_x = gelu_and_slope(mm(extra, up_ref[...]))
    slopes[q, :CROWS] = slope
    slopes[q, CROWS:] = slope_x
    total = mm(gate[:, :CROWS], act) + mm(gate[:, CROWS : CROWS + MAIN], act_x)
    acts[q] = total.astype(BF16)


def wide_of(i):
    return (i % (NE // 2)) * 2 + i // (NE // 2)


def sequence_order(w_here, transposed):
    n = 16 * NE
    a, b = (1, 0) if transposed else (0, 1)
    r, c = iota((n, n), a), iota((n, n), b)
    j = ((w_here + NE - wide_of(r // 16)) * UNSTRIDE) % NE
    row = ((r % 8) * CHUNKS + j // SIZE) * 16 + ((r // 8) % 2) * 8 + j % SIZE
    return onehot(c == row)


def late_order(w_here):
    pieces, count = D // 128, CHUNKS * 2 * SIZE
    r, c = iota((NE * 16, pieces * count), 0), iota((NE * 16, pieces * count), 1)
    j = ((w_here + NE - wide_of(r // 16)) * UNSTRIDE) % NE
    kind, piece = (r % 16) // pieces, (r % 16) % pieces
    source = piece * count + (j // SIZE) * (2 * SIZE) + kind * SIZE + j % SIZE
    return onehot((c == source) & (kind < 2))


def late_rows(order, acts, down):
    pieces, count = D // 128, CHUNKS * 2 * SIZE
    part = mm(acts.reshape(count, FB), down).astype(BF16)
    stacked = jnp.concatenate([part[:, k * 128 : (k + 1) * 128] for k in range(pieces)], axis=0)
    return mm(order, stacked).reshape(2, NE // 2, 16, 128)


def split(v):
    high = v.astype(BF16)
    return high, (v - high.astype(F32)).astype(BF16)


def targets(positive):
    pairs = 8 * NE

    def number(j):
        return wide_of(j // 8) * 8 + j % 8

    r, c = iota((pairs, pairs), 0), iota((pairs, pairs), 1)
    return mm(onehot(number(r) == c), onehot(number(r) == positive), 1, 1)


def row_gradients(pooled, target):
    pairs = 8 * NE
    query = pooled[:, :8].reshape(pairs, D)
    document = pooled[:, 8:].reshape(pairs, D)
    query_b, document_b = query.astype(BF16), document.astype(BF16)
    inverse_q = lax.rsqrt(jnp.sum(query * query, axis=-1, keepdims=True) + EPS)
    inverse_d = lax.rsqrt(jnp.sum(document * document, axis=-1, keepdims=True) + EPS)
    squares = mm(jnp.ones((8, D), F32), document * document, 1, 1, HIGHEST)
    inverse_row = lax.rsqrt(squares[0:1] + EPS)
    weights = jnp.exp(mm(query_b, document_b, 1, 1) * (inverse_q * WARMTH) * inverse_row)
    probs = weights / jnp.sum(weights, axis=1, keepdims=True)

    excess = (probs - target) * (LOSS_SCALE * WARMTH)
    high, rest = split(excess * inverse_row)
    grad_q = mm(high, document_b) + mm(rest, document_b)
    high, rest = split(excess * inverse_q)
    grad_d = mm(high, query_b, 0, 0) + mm(rest, query_b, 0, 0)

    def back(row, grad, inverse):
        unit = row * inverse
        inner = jnp.sum(unit * grad, axis=-1, keepdims=True)
        return ((grad - unit * inner) * (inverse * (1.0 / SEQ))).reshape(NE, 8, D)

    both = [back(query, grad_q, inverse_q), back(document, grad_d, inverse_d)]
    return jnp.concatenate(both, axis=1).reshape(16 * NE, D).astype(BF16)


def each(start, stop, act):
    def one(i, carry):
        act(i)
        return carry

    lax.fori_loop(start, stop, one, 0)


def step_kernel(
    nw, nz,
    x_ref, ids_ref, positive_ref, wr_ref, wqkv_hbm, wout_hbm, up_hbm, down_hbm,
    grad_up_ref, grad_down_ref,
    wqkv_ref, wout_ref, up_ref, down_ref, load_sems,
    blocks, mixed, rows, sides, turned, extras, slopes, gates, acts, spread, dpre_x,
    order, order_back, order_late, target, ordered, part, lent, half, got, late_all, late_lent, late_half, late_send, late_got, zsend, zgot, pooled,
    s1, r1, s2, r2, sem_core, s3, r3, s4, r4, s5, r5, s6, r6, s7, r7,
):
    w, z = lax.axis_index("wide"), lax.axis_index("narrow")
    right, left = lax.rem(z + 1, nz), lax.rem(z + nz - 1, nz)
    hops, chips = nz // 2, nw // 2
    chip, core = w // 2, lax.rem(w, 2)
    sibling = w + 1 - 2 * core

    class loads:
        steps = [
            [
                (
                    wqkv_hbm.at[:, pl.ds(third * D + block * 256, 256)],
                    wqkv_ref.at[:, pl.ds(third * D + block * 256, 256)],
                )
                for third in range(3)
            ]
            for block in range(D // 256)
        ] + [[(wout_hbm, wout_ref)], [(up_hbm, up_ref)], [(down_hbm, down_ref)]]

        def copies(step):
            return [
                pltpu.make_async_copy(source, target, load_sems.at[step, i])
                for i, (source, target) in enumerate(loads.steps[step])
            ]

        def start(step):
            for one in loads.copies(step):
                one.start()

        def wait(step):
            for one in loads.copies(step):
                one.wait()

    for step in range(len(loads.steps)):
        loads.start(step)

    barrier = pltpu.get_barrier_semaphore()

    def greet(peer):
        pl.semaphore_signal(barrier, inc=1, device_id=peer, device_id_type=MESH)

    each(1, nw, lambda d: greet((lax.rem(w + d, nw), z)))
    each(1, nz, lambda d: greet((w, lax.rem(z + d, nz))))

    mean_q, mean_d = front(
        loads, x_ref, ids_ref, wqkv_ref, wout_ref, wr_ref, blocks, mixed
    )
    for step in (-2, -1):
        loads.wait(len(loads.steps) + step)

    pl.semaphore_wait(barrier, nw + nz - 2)

    def copy(source, target, send, receive, peer):
        return pltpu.make_async_remote_copy(
            src_ref=source, dst_ref=target, send_sem=send, recv_sem=receive,
            device_id=peer, device_id_type=MESH,
        )

    def first(j):
        peer = lax.rem(w + STRIDE * j, nw)
        return copy(blocks.at[peer], rows.at[z, j], s1.at[j], r1.at[j], (peer, z))

    def send_chunk(c):
        each(jnp.maximum(c * SIZE, 1), (c + 1) * SIZE, lambda j: first(j).start())

    def onward(way, j):
        block = rows.at[z, j, :, pl.ds(0, D)]
        c = j // SIZE
        return copy(
            block, block, s2.at[way, 0, c, 0], r2.at[way, 0, c, 0],
            (w, right if way == 0 else left),
        )

    def arrived(c):
        def one(j):
            pltpu.make_async_copy(blocks.at[j], rows.at[z, j], r1.at[j]).wait()
            for way in range(2):
                onward(way, j).start()

        each(c * SIZE, (c + 1) * SIZE, one)

    class move:
        def __init__(self, way, hop, c, items=(0, 1)):
            plane = lax.rem(z + nz + (2 * way - 1) * (hop - 1), nz)
            main = rows.at[plane, pl.ds(c * SIZE, SIZE), :, pl.ds(0, D)]
            blocks = (main, sides.at[plane * CHUNKS + c])
            self.copies = [
                copy(
                    blocks[i], blocks[i], s2.at[way, hop - 1, c, i], r2.at[way, hop - 1, c, i],
                    (w, right if way == 0 else left),
                )
                for i in items
            ]

        def start(self):
            for one in self.copies:
                one.start()

        def wait_recv(self):
            for one in self.copies:
                one.wait_recv()

        def wait_send(self):
            for one in self.copies:
                one.wait_send()

    def work(plane, c):
        expert_chunk(plane, c, rows, sides, up_ref, turned, extras, slopes, gates, acts)

    def work_both(hop, c):
        each(0, 2, lambda way: work(lax.rem(z + nz + (2 * way - 1) * hop, nz), c))

    pltpu.make_async_copy(blocks.at[w], rows.at[z, 0], r1.at[0]).start()
    each(0, CHUNKS, send_chunk)

    def home(c):
        arrived(c)
        sides[z * CHUNKS + c] = pack_side(rows[z, pl.ds(c * SIZE, SIZE), :, D:])
        for way in range(2):
            move(way, 1, c, (1,)).start()

    each(0, CHUNKS, home)

    order[...] = sequence_order(w, False)
    order_back[...] = sequence_order(w, True)
    order_late[...] = late_order(w)
    target[...] = targets(positive_ref[...])

    def both_ways(hop, c, onward, behind):
        for way in range(2):
            move(way, hop, c).wait_recv()
            if way in onward:
                move(way, hop + 1, c).start()
        behind(c)

    each(0, CHUNKS, lambda c: both_ways(1, c, (0, 1), lambda c: work(z, c)))
    each(0, (hops - 3) * CHUNKS, lambda i: both_ways(
        2 + i // CHUNKS, lax.rem(i, CHUNKS), (0, 1), lambda c: work_both(1 + i // CHUNKS, c)
    ))
    half_way = CHUNKS // 2
    each(0, half_way, lambda c: both_ways(hops - 1, c, (0,), lambda c: work_both(hops - 2, c)))
    each(half_way, CHUNKS, lambda c: both_ways(hops - 1, c, (1,), lambda c: work_both(hops - 2, c)))
    each(0, CHUNKS, lambda c: work_both(hops - 1, c))

    far = lax.rem(z + hops, nz)
    acts[pl.ds(far * CHUNKS, CHUNKS)] = jnp.zeros((CHUNKS, 2 * SIZE, FB), BF16)
    side = NE // 2 * 16
    ordered[...] = mm(order[...], acts[...].reshape(16 * NE, FB)).astype(BF16)

    def partial(which):
        return mm(ordered[pl.ds(pl.multiple_of(which * side, side), side)], down_ref[...])

    lent[...] = partial(1 - core).astype(BF16).reshape(lent.shape)
    swap = copy(lent, half, sem_core.at[0], sem_core.at[1], (sibling, z))
    swap.start()
    part[...] = partial(core).reshape(part.shape)
    swap.wait_recv()
    part[...] = part[...] + half[...].astype(F32)
    swap.wait_send()
    lent[...] = part[...].astype(BF16)

    def peer_chip(d):
        return lax.rem(chip + d, chips)

    def scatter(d):
        return copy(
            lent.at[peer_chip(d)], got.at[d], s3.at[d], r3.at[d], (peer_chip(d) * 2 + core, z)
        )

    def across(d):
        return copy(zsend, zgot.at[d], s4.at[d], r4.at[d], (w, lax.rem(z + d, nz)))

    def gather(d, origin):
        block = pooled.at[core, origin]
        return copy(block, block, s5.at[d], r5.at[d], (peer_chip(d) * 2 + core, z))

    def lend(d, origin, holder):
        block = pooled.at[holder, origin]
        return copy(block, block, s6.at[d], r6.at[d], (sibling, z))

    each(1, chips, lambda d: scatter(d).start())

    def last(i):
        for way in range(2):
            move(way, hops, i + way * half_way).wait_recv()
        for way in range(2):
            work(lax.rem(z + hops, nz), i + way * half_way)

    each(0, half_way, last)

    def summed(count, one_copy, buffer, start):
        def one(d, total):
            one_copy(d).wait_recv()
            return total + buffer[d].astype(F32)

        return lax.fori_loop(1, count, one, start)

    late_all[...] = late_rows(order_late[...], acts[pl.ds(far * CHUNKS, CHUNKS)], down_ref[...])
    late_lent[...] = late_all[1 - core].astype(BF16)
    late_swap = copy(late_lent, late_half, sem_core.at[2], sem_core.at[3], (sibling, z))
    late_swap.start()
    late_swap.wait_recv()
    late_part = late_all[core] + late_half[...].astype(F32)
    late_all[core] = late_part
    late_send[...] = late_part.astype(BF16)

    def late_scatter(d):
        return copy(
            late_send.at[peer_chip(d)], late_got.at[d], s7.at[d], r7.at[d],
            (peer_chip(d) * 2 + core, z),
        )

    each(1, chips, lambda d: late_scatter(d).start())
    total = summed(chips, scatter, got, part[chip])
    late = summed(chips, late_scatter, late_got, late_all[core, chip])
    row = iota((16, 1), 0)
    pieces = D // 128
    total = total + jnp.concatenate(
        [
            jnp.where(row == far, late[k : k + 1], 0.0)
            + jnp.where(row == far + 8, late[pieces + k : pieces + k + 1], 0.0)
            for k in range(pieces)
        ],
        axis=1,
    )
    total = total * (1.0 / SEQ)
    total = total + jnp.where(row == z, mean_q, 0.0) + jnp.where(row == z + 8, mean_d, 0.0)
    zsend[...] = total.astype(BF16)
    each(1, nz, lambda d: across(d).start())
    ordered[...] = mm(order[...], acts[...].reshape(16 * NE, FB)).astype(BF16)
    pooled[core, chip] = summed(nz, across, zgot, total).astype(BF16)
    each(1, chips, lambda d: gather(d, chip).start())
    lend(0, chip, core).start()

    def pass_on(d):
        origin = lax.rem(chip - d + chips, chips)
        gather(d, origin).wait_recv()
        lend(d, origin, core).start()

    each(1, chips, pass_on)
    each(0, chips, lambda d: lend(d, lax.rem(chip - d + chips, chips), 1 - core).wait_recv())

    dy = row_gradients(pooled[...].reshape(NE, 16, D).astype(F32), target[...])
    grad_down_ref[...] = mm(ordered[...], dy, 0, 0)
    back = mm(dy, down_ref[...], 1, 1).astype(BF16)
    spread[...] = mm(order_back[...], back).astype(BF16).reshape(spread.shape)

    grad_up_ref[...] = jnp.zeros_like(grad_up_ref)

    def add(p):
        left_side, right_side = [], []
        for c in range(CHUNKS):
            q = p * CHUNKS + c
            product = mm(gates[q], spread[q]) * slopes[q].astype(F32)
            right_side.append(product[:CROWS].astype(BF16))
            dpre_x[q] = product[CROWS:].astype(BF16)
            left_side.append(turned[q])
        grad_up_ref[...] += mm(
            jnp.concatenate(left_side, axis=1), jnp.concatenate(right_side, axis=0)
        )

    each(0, nz, add)
    extra_rows = nz * CHUNKS * MAIN
    grad_up_ref[...] += mm(
        extras[...].reshape(extra_rows, D), dpre_x[...].reshape(extra_rows, FB), 0, 0
    )

    each(1, nw, lambda j: first(j).wait_send())
    for way in range(2):
        each(0, (hops - 1) * CHUNKS, lambda i: move(way, 1 + i // CHUNKS, lax.rem(i, CHUNKS)).wait_send())
        each(0, CHUNKS // 2, lambda i: move(way, hops, i + way * (CHUNKS // 2)).wait_send())
    each(1, chips, lambda d: scatter(d).wait_send())
    late_swap.wait_send()
    each(1, chips, lambda d: late_scatter(d).wait_send())
    each(1, nz, lambda d: across(d).wait_send())
    each(1, chips, lambda d: gather(d, chip).wait_send())
    each(0, chips, lambda d: lend(d, lax.rem(chip - d + chips, chips), core).wait_send())


def body(pair_tokens, expert_ids, positive, w_qkv, w_out, w_router, w_up, w_down):
    nw, nz = lax.axis_size("wide"), lax.axis_size("narrow")
    chips, parts = nw // 2, nz * CHUNKS
    dma = pltpu.SemaphoreType.DMA
    vmem = pl.BlockSpec(memory_space=pltpu.VMEM)
    grad_up, grad_down = pl.pallas_call(
        functools.partial(step_kernel, nw, nz),
        out_shape=(
            jax.ShapeDtypeStruct((D, FB), F32),
            jax.ShapeDtypeStruct((FB, D), F32),
        ),
        in_specs=[vmem] * 4 + [pl.BlockSpec(memory_space=pl.ANY)] * 4,
        out_specs=(vmem, vmem),
        scratch_shapes=[
            pltpu.VMEM(w_qkv.shape, BF16),
            pltpu.VMEM(w_out.shape, BF16),
            pltpu.VMEM((D, FB), BF16),
            pltpu.VMEM((FB, D), BF16),
            dma((D // 256 + 3, 3)),
            pltpu.VMEM((NE, MAIN, ROW), BF16),
            pltpu.VMEM((TOK, D), BF16),
            pltpu.VMEM((nz, nw, MAIN, ROW), BF16),
            pltpu.VMEM((parts, SROWS, 128), BF16),
            pltpu.VMEM((parts, D, CROWS), BF16),
            pltpu.VMEM((parts, MAIN, D), BF16),
            pltpu.VMEM((parts, CROWS + MAIN, FB), BF16),
            pltpu.VMEM((parts, CROWS + MAIN, 2 * SIZE), BF16),
            pltpu.VMEM((parts, 2 * SIZE, FB), BF16),
            pltpu.VMEM((parts, 2 * SIZE, FB), BF16),
            pltpu.VMEM((parts, MAIN, FB), BF16),
            pltpu.VMEM((16 * NE, 16 * NE), BF16),
            pltpu.VMEM((16 * NE, 16 * NE), BF16),
            pltpu.VMEM((16 * NE, D // 128 * CHUNKS * 2 * SIZE), BF16),
            pltpu.VMEM((8 * NE, 8 * NE), F32),
            pltpu.VMEM((16 * NE, FB), BF16),
            pltpu.VMEM((chips, 16, D), F32),
            pltpu.VMEM((chips, 16, D), BF16),
            pltpu.VMEM((chips, 16, D), BF16),
            pltpu.VMEM((chips, 16, D), BF16),
            pltpu.VMEM((2, chips, 16, 128), F32),
            pltpu.VMEM((chips, 16, 128), BF16),
            pltpu.VMEM((chips, 16, 128), BF16),
            pltpu.VMEM((chips, 16, 128), BF16),
            pltpu.VMEM((chips, 16, 128), BF16),
            pltpu.VMEM((16, D), BF16),
            pltpu.VMEM((nz, 16, D), BF16),
            pltpu.VMEM((2, chips, 16, D), BF16),
            dma((nw,)), dma((nw,)),
            dma((2, nz // 2, CHUNKS, 2)), dma((2, nz // 2, CHUNKS, 2)),
            dma((4,)),
            dma((chips,)), dma((chips,)),
            dma((nz,)), dma((nz,)),
            dma((chips,)), dma((chips,)),
            dma((chips,)), dma((chips,)),
            dma((chips,)), dma((chips,)),
        ],
        compiler_params=pltpu.CompilerParams(
            collective_id=0, has_side_effects=True, vmem_limit_bytes=VMEM_BYTES
        ),
        name="contrastive_step",
    )(
        pair_tokens.reshape(TOK, D),
        expert_ids.reshape(TOK, 2).T,
        positive.reshape(1, -1),
        w_router.T,
        w_qkv,
        w_out,
        w_up[0],
        w_down[0],
    )
    return (grad_up[None], grad_down[None])


def solution(mesh):
    return jax.shard_map(
        body,
        mesh=mesh,
        in_specs=(
            P(("wide", "narrow"), None, None, None),
            P(("wide", "narrow"), None, None),
            P(),
            P(),
            P(),
            P(),
            P("wide", None, "narrow"),
            P("wide", "narrow", None),
        ),
        out_specs=(P("wide", None, "narrow"), P("wide", "narrow", None)),
        check_vma=False,
    )
```

```python
import functools

import jax
import jax.numpy as jnp
from jax import lax
from jax.experimental import pallas as pl
from jax.experimental.pallas import tpu as pltpu
from jax.sharding import PartitionSpec as P

D = 768
FB = 384
SEQ = 128
TOK = 256
NE = 32
MAIN = 16
ROW = D + 128
CHUNKS = 4
SIZE = NE // CHUNKS
CROWS = SIZE * MAIN
SROWS = SIZE * 8
STRIDE, UNSTRIDE = 11, 3
EPS = 1e-06
WARMTH = 20.0
LOSS_SCALE = 64.0
VMEM_BYTES = 56 * 2**20
MESH = pl.DeviceIdType.MESH
HIGHEST = lax.Precision.HIGHEST
F32, BF16, I32 = jnp.float32, jnp.bfloat16, jnp.int32


def mm(a, b, ca=1, cb=0, precision=None):
    return lax.dot_general(
        a, b, (((ca,), (cb,)), ((), ())), precision=precision, preferred_element_type=F32
    )


def iota(shape, axis):
    return lax.broadcasted_iota(I32, shape, axis)


def onehot(condition):
    return jnp.where(condition, 1.0, 0.0).astype(BF16)


def rms(v):
    return v * lax.rsqrt(jnp.mean(v * v, axis=-1, keepdims=True) + EPS)


def front(loads, x_ref, ids_ref, wqkv_ref, wout_ref, wr_ref, blocks, mixed):
    normed = rms(x_ref[...].astype(F32)).astype(BF16)
    wide = 256
    same_head = onehot(iota((wide, wide), 0) // 64 == iota((wide, wide), 1) // 64)
    low = iota((SEQ, 128), 1) < 64
    ones = jnp.ones((SEQ, 128), BF16)

    def head_rms(v):
        square = v * v
        high = square.astype(BF16)
        rest = (square - high.astype(F32)).astype(BF16)
        mean = (mm(high, same_head) + mm(rest, same_head)) * (1.0 / 64.0)
        return (v * lax.rsqrt(mean + EPS)).astype(BF16)

    for block in range(D // wide):
        at = block * wide
        loads.wait(block)
        q = head_rms(mm(normed, wqkv_ref[:, at : at + wide]))
        k = head_rms(mm(normed, wqkv_ref[:, D + at : D + at + wide]))
        v = mm(normed, wqkv_ref[:, 2 * D + at : 2 * D + at + wide]).astype(BF16)
        for s in range(TOK // SEQ):
            rows = slice(s * SEQ, (s + 1) * SEQ)
            for c in range(wide // 128):
                lanes = slice(c * 128, (c + 1) * 128)
                qc, kc = q[rows, lanes], k[rows, lanes]
                values = jnp.concatenate([v[rows, lanes], ones], axis=1)
                heads = []
                for half in range(2):
                    qh = jnp.where(low if half == 0 else ~low, qc, jnp.zeros_like(qc))
                    weights = jnp.exp(mm(qh, kc, 1, 1) * 0.125).astype(BF16)
                    both = mm(weights, values)
                    heads.append(both[:, :128] / both[:, 128:])
                mixed[rows, at + c * 128 : at + (c + 1) * 128] = jnp.where(
                    low, heads[0], heads[1]
                ).astype(BF16)

    loads.wait(D // wide)
    h = (x_ref[...].astype(F32) + mm(mixed[...], wout_ref[...])).astype(BF16).astype(F32)
    mean_q = jnp.mean(h[:SEQ], axis=0, keepdims=True)
    mean_d = jnp.mean(h[SEQ:], axis=0, keepdims=True)
    z = rms(h).astype(BF16)

    logits = mm(wr_ref[...], z, 1, 1)
    names = iota((NE, TOK), 0)
    here = (ids_ref[0:1, :] == names) | (ids_ref[1:2, :] == names)
    earlier = onehot(iota((TOK, TOK), 0) < iota((TOK, TOK), 1))
    rank = jnp.where(here, mm(onehot(here), earlier), -1.0)
    both_logits = jnp.sum(jnp.where(here, logits, 0.0), axis=0, keepdims=True)
    gate = jnp.where(here, 1.0 / (1.0 + jnp.exp(both_logits - 2.0 * logits)), 0.0)

    spread = onehot(iota((NE * MAIN, NE), 0) // MAIN == iota((NE * MAIN, NE), 1))
    slot = (iota((NE * MAIN, TOK), 0) % MAIN).astype(F32)
    main = mm(onehot(mm(spread, rank.astype(BF16)) == slot), z).astype(BF16)
    blocks[:, :, :D] = main.reshape(NE, MAIN, D)

    extra = mm(onehot(rank == float(MAIN)), z).astype(BF16)
    lane = iota((NE, 128), 1)
    gates_q = jnp.zeros((NE, 128), F32)
    gates_d = jnp.zeros((NE, 128), F32)
    for s in range(MAIN + 1):
        chosen = jnp.where(rank == float(s), gate, 0.0)
        gates_q = jnp.where(lane == s, jnp.sum(chosen[:, :SEQ], axis=1, keepdims=True), gates_q)
        gates_d = jnp.where(lane == s, jnp.sum(chosen[:, SEQ:], axis=1, keepdims=True), gates_d)
    parts = [extra[:, c * 128 : (c + 1) * 128] for c in range(D // 128)]
    stacked = jnp.concatenate(parts + [gates_q.astype(BF16), gates_d.astype(BF16)], axis=0)
    r, c = iota((NE * MAIN, 8 * NE), 0), iota((NE * MAIN, 8 * NE), 1)
    side = mm(onehot(c == (r % MAIN) * NE + r // MAIN), stacked).astype(BF16)
    blocks[:, :, D:] = side.reshape(NE, MAIN, 128)
    return mean_q, mean_d


def gelu_and_slope(x):
    a, b = 0.7978845608028654, 0.044715
    square = x * x
    t = jnp.tanh(a * x * (1.0 + b * square))
    half = 0.5 * (1.0 + t)
    slope = half + 0.5 * x * (1.0 - t * t) * (a * (1.0 + 3.0 * b * square))
    return (x * half).astype(BF16), slope.astype(BF16)


def pack_side(block):
    r, col = iota((SROWS, CROWS), 0), iota((SROWS, CROWS), 1)
    take = onehot(col == (r % SIZE) * MAIN + r // SIZE)
    return mm(take, block.reshape(CROWS, 128)).astype(BF16)


def expert_chunk(plane, c, rows, sides, up_ref, turned, extras, slopes, gates, acts):
    q = plane * CHUNKS + c
    main = rows[plane, pl.ds(c * SIZE, SIZE)].reshape(CROWS, ROW)[:, :D]
    turned[q] = main.T
    side = sides[q].astype(F32)
    extra = jnp.concatenate(
        [side[k * SIZE : (k + 1) * SIZE] for k in range(D // 128)], axis=1
    )
    extra = jnp.concatenate([extra, jnp.zeros((MAIN - SIZE, D), F32)]).astype(BF16)
    extras[q] = extra
    own = side[6 * SIZE :]
    wide = CROWS + 128
    s, j = iota((128, wide), 0), iota((128, wide), 1)
    repeat = onehot(s == jnp.where(j < CROWS, j % MAIN, MAIN))
    i, j = iota((2 * SIZE, wide), 0), iota((2 * SIZE, wide), 1)
    mine = jnp.where(j < CROWS, j // MAIN, j - CROWS) == i % SIZE
    gate = jnp.where(mine, mm(own.astype(BF16), repeat), 0.0).astype(BF16)
    gates[q] = gate[:, : CROWS + MAIN].T
    act, slope = gelu_and_slope(mm(main, up_ref[...]))
    act_x, slope_x = gelu_and_slope(mm(extra, up_ref[...]))
    slopes[q, :CROWS] = slope
    slopes[q, CROWS:] = slope_x
    total = mm(gate[:, :CROWS], act) + mm(gate[:, CROWS : CROWS + MAIN], act_x)
    acts[q] = total.astype(BF16)


def wide_of(i):
    return (i % (NE // 2)) * 2 + i // (NE // 2)


def sequence_order(w_here, transposed):
    n = 16 * NE
    a, b = (1, 0) if transposed else (0, 1)
    r, c = iota((n, n), a), iota((n, n), b)
    j = ((w_here + NE - wide_of(r // 16)) * UNSTRIDE) % NE
    row = ((r % 8) * CHUNKS + j // SIZE) * 16 + ((r // 8) % 2) * 8 + j % SIZE
    return onehot(c == row)


def late_order(w_here):
    pieces, count = D // 128, CHUNKS * 2 * SIZE
    r, c = iota((NE * 16, pieces * count), 0), iota((NE * 16, pieces * count), 1)
    j = ((w_here + NE - wide_of(r // 16)) * UNSTRIDE) % NE
    kind, piece = (r % 16) // pieces, (r % 16) % pieces
    source = piece * count + (j // SIZE) * (2 * SIZE) + kind * SIZE + j % SIZE
    return onehot((c == source) & (kind < 2))


def late_rows(order, acts, down):
    pieces, count = D // 128, CHUNKS * 2 * SIZE
    part = mm(acts.reshape(count, FB), down).astype(BF16)
    stacked = jnp.concatenate([part[:, k * 128 : (k + 1) * 128] for k in range(pieces)], axis=0)
    return mm(order, stacked).reshape(2, NE // 2, 16, 128)


def split(v):
    high = v.astype(BF16)
    return high, (v - high.astype(F32)).astype(BF16)


def targets(positive):
    pairs = 8 * NE

    def number(j):
        return wide_of(j // 8) * 8 + j % 8

    r, c = iota((pairs, pairs), 0), iota((pairs, pairs), 1)
    return mm(onehot(number(r) == c), onehot(number(r) == positive), 1, 1)


def row_gradients(pooled, target):
    pairs = 8 * NE
    query = pooled[:, :8].reshape(pairs, D)
    document = pooled[:, 8:].reshape(pairs, D)
    query_b, document_b = query.astype(BF16), document.astype(BF16)
    inverse_q = lax.rsqrt(jnp.sum(query * query, axis=-1, keepdims=True) + EPS)
    inverse_d = lax.rsqrt(jnp.sum(document * document, axis=-1, keepdims=True) + EPS)
    squares = mm(jnp.ones((8, D), F32), document * document, 1, 1, HIGHEST)
    inverse_row = lax.rsqrt(squares[0:1] + EPS)
    weights = jnp.exp(mm(query_b, document_b, 1, 1) * (inverse_q * WARMTH) * inverse_row)
    probs = weights / jnp.sum(weights, axis=1, keepdims=True)

    excess = (probs - target) * (LOSS_SCALE * WARMTH)
    high, rest = split(excess * inverse_row)
    grad_q = mm(high, document_b) + mm(rest, document_b)
    high, rest = split(excess * inverse_q)
    grad_d = mm(high, query_b, 0, 0) + mm(rest, query_b, 0, 0)

    def back(row, grad, inverse):
        unit = row * inverse
        inner = jnp.sum(unit * grad, axis=-1, keepdims=True)
        return ((grad - unit * inner) * (inverse * (1.0 / SEQ))).reshape(NE, 8, D)

    both = [back(query, grad_q, inverse_q), back(document, grad_d, inverse_d)]
    return jnp.concatenate(both, axis=1).reshape(16 * NE, D).astype(BF16)


def each(start, stop, act):
    def one(i, carry):
        act(i)
        return carry

    lax.fori_loop(start, stop, one, 0)


def step_kernel(
    nw, nz,
    x_ref, ids_ref, positive_ref, wr_ref, wqkv_hbm, wout_hbm, up_hbm, down_hbm,
    grad_up_ref, grad_down_ref,
    wqkv_ref, wout_ref, up_ref, down_ref, load_sems,
    blocks, mixed, rows, sides, turned, extras, slopes, gates, acts, spread, dpre_x,
    order, order_back, order_late, target, turned_acts, turned_extras, ordered, part, lent, half, got, late_all, late_lent, late_half, late_send, late_got, zsend, zgot, pooled,
    s1, r1, s2, r2, sem_core, s3, r3, s4, r4, s5, r5, s6, r6, s7, r7,
):
    w, z = lax.axis_index("wide"), lax.axis_index("narrow")
    right, left = lax.rem(z + 1, nz), lax.rem(z + nz - 1, nz)
    hops, chips = nz // 2, nw // 2
    chip, core = w // 2, lax.rem(w, 2)
    sibling = w + 1 - 2 * core

    class loads:
        steps = [
            [
                (
                    wqkv_hbm.at[:, pl.ds(third * D + block * 256, 256)],
                    wqkv_ref.at[:, pl.ds(third * D + block * 256, 256)],
                )
                for third in range(3)
            ]
            for block in range(D // 256)
        ] + [[(wout_hbm, wout_ref)], [(up_hbm, up_ref)], [(down_hbm, down_ref)]]

        def copies(step):
            return [
                pltpu.make_async_copy(source, target, load_sems.at[step, i])
                for i, (source, target) in enumerate(loads.steps[step])
            ]

        def start(step):
            for one in loads.copies(step):
                one.start()

        def wait(step):
            for one in loads.copies(step):
                one.wait()

    for step in range(len(loads.steps)):
        loads.start(step)

    barrier = pltpu.get_barrier_semaphore()

    def greet(peer):
        pl.semaphore_signal(barrier, inc=1, device_id=peer, device_id_type=MESH)

    each(1, nw, lambda d: greet((lax.rem(w + d, nw), z)))
    each(1, nz, lambda d: greet((w, lax.rem(z + d, nz))))

    mean_q, mean_d = front(
        loads, x_ref, ids_ref, wqkv_ref, wout_ref, wr_ref, blocks, mixed
    )
    for step in (-2, -1):
        loads.wait(len(loads.steps) + step)

    pl.semaphore_wait(barrier, nw + nz - 2)

    def copy(source, target, send, receive, peer):
        return pltpu.make_async_remote_copy(
            src_ref=source, dst_ref=target, send_sem=send, recv_sem=receive,
            device_id=peer, device_id_type=MESH,
        )

    def first(j):
        peer = lax.rem(w + STRIDE * j, nw)
        return copy(blocks.at[peer], rows.at[z, j], s1.at[j], r1.at[j], (peer, z))

    def send_chunk(c):
        each(jnp.maximum(c * SIZE, 1), (c + 1) * SIZE, lambda j: first(j).start())

    def onward(way, j):
        block = rows.at[z, j, :, pl.ds(0, D)]
        c = j // SIZE
        return copy(
            block, block, s2.at[way, 0, c, 0], r2.at[way, 0, c, 0],
            (w, right if way == 0 else left),
        )

    def arrived(c):
        def one(j):
            pltpu.make_async_copy(blocks.at[j], rows.at[z, j], r1.at[j]).wait()
            for way in range(2):
                onward(way, j).start()

        each(c * SIZE, (c + 1) * SIZE, one)

    class move:
        def __init__(self, way, hop, c, items=(0, 1)):
            plane = lax.rem(z + nz + (2 * way - 1) * (hop - 1), nz)
            main = rows.at[plane, pl.ds(c * SIZE, SIZE), :, pl.ds(0, D)]
            blocks = (main, sides.at[plane * CHUNKS + c])
            self.copies = [
                copy(
                    blocks[i], blocks[i], s2.at[way, hop - 1, c, i], r2.at[way, hop - 1, c, i],
                    (w, right if way == 0 else left),
                )
                for i in items
            ]

        def start(self):
            for one in self.copies:
                one.start()

        def wait_recv(self):
            for one in self.copies:
                one.wait_recv()

        def wait_send(self):
            for one in self.copies:
                one.wait_send()

    def work(plane, c):
        expert_chunk(plane, c, rows, sides, up_ref, turned, extras, slopes, gates, acts)

    def work_both(hop, c):
        each(0, 2, lambda way: work(lax.rem(z + nz + (2 * way - 1) * hop, nz), c))

    pltpu.make_async_copy(blocks.at[w], rows.at[z, 0], r1.at[0]).start()
    each(0, CHUNKS, send_chunk)

    def home(c):
        arrived(c)
        sides[z * CHUNKS + c] = pack_side(rows[z, pl.ds(c * SIZE, SIZE), :, D:])
        for way in range(2):
            move(way, 1, c, (1,)).start()

    each(0, CHUNKS, home)

    order[...] = sequence_order(w, False)
    order_back[...] = sequence_order(w, True)
    order_late[...] = late_order(w)
    target[...] = targets(positive_ref[...])

    def both_ways(hop, c, onward, behind):
        for way in range(2):
            move(way, hop, c).wait_recv()
            if way in onward:
                move(way, hop + 1, c).start()
        behind(c)

    each(0, CHUNKS, lambda c: both_ways(1, c, (0, 1), lambda c: work(z, c)))
    each(0, (hops - 3) * CHUNKS, lambda i: both_ways(
        2 + i // CHUNKS, lax.rem(i, CHUNKS), (0, 1), lambda c: work_both(1 + i // CHUNKS, c)
    ))
    half_way = CHUNKS // 2
    each(0, half_way, lambda c: both_ways(hops - 1, c, (0,), lambda c: work_both(hops - 2, c)))
    each(half_way, CHUNKS, lambda c: both_ways(hops - 1, c, (1,), lambda c: work_both(hops - 2, c)))
    each(0, CHUNKS, lambda c: work_both(hops - 1, c))

    far = lax.rem(z + hops, nz)
    acts[pl.ds(far * CHUNKS, CHUNKS)] = jnp.zeros((CHUNKS, 2 * SIZE, FB), BF16)
    side = NE // 2 * 16
    ordered[...] = mm(order[...], acts[...].reshape(16 * NE, FB)).astype(BF16)

    def partial(which):
        return mm(ordered[pl.ds(pl.multiple_of(which * side, side), side)], down_ref[...])

    lent[...] = partial(1 - core).astype(BF16).reshape(lent.shape)
    swap = copy(lent, half, sem_core.at[0], sem_core.at[1], (sibling, z))
    swap.start()
    part[...] = partial(core).reshape(part.shape)
    swap.wait_recv()
    part[...] = part[...] + half[...].astype(F32)
    swap.wait_send()
    lent[...] = part[...].astype(BF16)

    def peer_chip(d):
        return lax.rem(chip + d, chips)

    def scatter(d):
        return copy(
            lent.at[peer_chip(d)], got.at[d], s3.at[d], r3.at[d], (peer_chip(d) * 2 + core, z)
        )

    def across(d):
        return copy(zsend, zgot.at[d], s4.at[d], r4.at[d], (w, lax.rem(z + d, nz)))

    def gather(d, origin):
        block = pooled.at[core, origin]
        return copy(block, block, s5.at[d], r5.at[d], (peer_chip(d) * 2 + core, z))

    def lend(d, origin, holder):
        block = pooled.at[holder, origin]
        return copy(block, block, s6.at[d], r6.at[d], (sibling, z))

    each(1, chips, lambda d: scatter(d).start())

    def last(i):
        for way in range(2):
            move(way, hops, i + way * half_way).wait_recv()
        for way in range(2):
            work(lax.rem(z + hops, nz), i + way * half_way)

    each(0, half_way, last)

    def summed(count, one_copy, buffer, start):
        def one(d, total):
            one_copy(d).wait_recv()
            return total + buffer[d].astype(F32)

        return lax.fori_loop(1, count, one, start)

    late_all[...] = late_rows(order_late[...], acts[pl.ds(far * CHUNKS, CHUNKS)], down_ref[...])
    late_lent[...] = late_all[1 - core].astype(BF16)
    late_swap = copy(late_lent, late_half, sem_core.at[2], sem_core.at[3], (sibling, z))
    late_swap.start()
    late_swap.wait_recv()
    late_part = late_all[core] + late_half[...].astype(F32)
    late_all[core] = late_part
    late_send[...] = late_part.astype(BF16)

    def late_scatter(d):
        return copy(
            late_send.at[peer_chip(d)], late_got.at[d], s7.at[d], r7.at[d],
            (peer_chip(d) * 2 + core, z),
        )

    each(1, chips, lambda d: late_scatter(d).start())
    total = summed(chips, scatter, got, part[chip])
    late = summed(chips, late_scatter, late_got, late_all[core, chip])
    row = iota((16, 1), 0)
    pieces = D // 128
    total = total + jnp.concatenate(
        [
            jnp.where(row == far, late[k : k + 1], 0.0)
            + jnp.where(row == far + 8, late[pieces + k : pieces + k + 1], 0.0)
            for k in range(pieces)
        ],
        axis=1,
    )
    total = total * (1.0 / SEQ)
    total = total + jnp.where(row == z, mean_q, 0.0) + jnp.where(row == z + 8, mean_d, 0.0)
    zsend[...] = total.astype(BF16)
    each(1, nz, lambda d: across(d).start())
    turned_acts[...] = mm(order[...], acts[...].reshape(16 * NE, FB)).astype(BF16).T
    turned_extras[...] = extras[...].reshape(turned_extras.shape[1], D).T
    pooled[core, chip] = summed(nz, across, zgot, total).astype(BF16)
    each(1, chips, lambda d: gather(d, chip).start())
    lend(0, chip, core).start()

    def pass_on(d):
        origin = lax.rem(chip - d + chips, chips)
        gather(d, origin).wait_recv()
        lend(d, origin, core).start()

    each(1, chips, pass_on)
    each(0, chips, lambda d: lend(d, lax.rem(chip - d + chips, chips), 1 - core).wait_recv())

    dy = row_gradients(pooled[...].reshape(NE, 16, D).astype(F32), target[...])
    grad_down_ref[...] = mm(turned_acts[...], dy)
    back = mm(dy, down_ref[...], 1, 1).astype(BF16)
    spread[...] = mm(order_back[...], back).astype(BF16).reshape(spread.shape)

    grad_up_ref[...] = jnp.zeros_like(grad_up_ref)

    def add(p):
        left_side, right_side = [], []
        for c in range(CHUNKS):
            q = p * CHUNKS + c
            product = mm(gates[q], spread[q]) * slopes[q].astype(F32)
            right_side.append(product[:CROWS].astype(BF16))
            dpre_x[q] = product[CROWS:].astype(BF16)
            left_side.append(turned[q])
        grad_up_ref[...] += mm(
            jnp.concatenate(left_side, axis=1), jnp.concatenate(right_side, axis=0)
        )

    each(0, nz, add)
    extra_rows = nz * CHUNKS * MAIN
    grad_up_ref[...] += mm(
        turned_extras[...], dpre_x[...].reshape(extra_rows, FB)
    )

    each(1, nw, lambda j: first(j).wait_send())
    for way in range(2):
        each(0, (hops - 1) * CHUNKS, lambda i: move(way, 1 + i // CHUNKS, lax.rem(i, CHUNKS)).wait_send())
        each(0, CHUNKS // 2, lambda i: move(way, hops, i + way * (CHUNKS // 2)).wait_send())
    each(1, chips, lambda d: scatter(d).wait_send())
    late_swap.wait_send()
    each(1, chips, lambda d: late_scatter(d).wait_send())
    each(1, nz, lambda d: across(d).wait_send())
    each(1, chips, lambda d: gather(d, chip).wait_send())
    each(0, chips, lambda d: lend(d, lax.rem(chip - d + chips, chips), core).wait_send())


def body(pair_tokens, expert_ids, positive, w_qkv, w_out, w_router, w_up, w_down):
    nw, nz = lax.axis_size("wide"), lax.axis_size("narrow")
    chips, parts = nw // 2, nz * CHUNKS
    dma = pltpu.SemaphoreType.DMA
    vmem = pl.BlockSpec(memory_space=pltpu.VMEM)
    grad_up, grad_down = pl.pallas_call(
        functools.partial(step_kernel, nw, nz),
        out_shape=(
            jax.ShapeDtypeStruct((D, FB), F32),
            jax.ShapeDtypeStruct((FB, D), F32),
        ),
        in_specs=[vmem] * 4 + [pl.BlockSpec(memory_space=pl.ANY)] * 4,
        out_specs=(vmem, vmem),
        scratch_shapes=[
            pltpu.VMEM(w_qkv.shape, BF16),
            pltpu.VMEM(w_out.shape, BF16),
            pltpu.VMEM((D, FB), BF16),
            pltpu.VMEM((FB, D), BF16),
            dma((D // 256 + 3, 3)),
            pltpu.VMEM((NE, MAIN, ROW), BF16),
            pltpu.VMEM((TOK, D), BF16),
            pltpu.VMEM((nz, nw, MAIN, ROW), BF16),
            pltpu.VMEM((parts, SROWS, 128), BF16),
            pltpu.VMEM((parts, D, CROWS), BF16),
            pltpu.VMEM((parts, MAIN, D), BF16),
            pltpu.VMEM((parts, CROWS + MAIN, FB), BF16),
            pltpu.VMEM((parts, CROWS + MAIN, 2 * SIZE), BF16),
            pltpu.VMEM((parts, 2 * SIZE, FB), BF16),
            pltpu.VMEM((parts, 2 * SIZE, FB), BF16),
            pltpu.VMEM((parts, MAIN, FB), BF16),
            pltpu.VMEM((16 * NE, 16 * NE), BF16),
            pltpu.VMEM((16 * NE, 16 * NE), BF16),
            pltpu.VMEM((16 * NE, D // 128 * CHUNKS * 2 * SIZE), BF16),
            pltpu.VMEM((8 * NE, 8 * NE), F32),
            pltpu.VMEM((FB, 16 * NE), BF16),
            pltpu.VMEM((D, parts * MAIN), BF16),
            pltpu.VMEM((16 * NE, FB), BF16),
            pltpu.VMEM((chips, 16, D), F32),
            pltpu.VMEM((chips, 16, D), BF16),
            pltpu.VMEM((chips, 16, D), BF16),
            pltpu.VMEM((chips, 16, D), BF16),
            pltpu.VMEM((2, chips, 16, 128), F32),
            pltpu.VMEM((chips, 16, 128), BF16),
            pltpu.VMEM((chips, 16, 128), BF16),
            pltpu.VMEM((chips, 16, 128), BF16),
            pltpu.VMEM((chips, 16, 128), BF16),
            pltpu.VMEM((16, D), BF16),
            pltpu.VMEM((nz, 16, D), BF16),
            pltpu.VMEM((2, chips, 16, D), BF16),
            dma((nw,)), dma((nw,)),
            dma((2, nz // 2, CHUNKS, 2)), dma((2, nz // 2, CHUNKS, 2)),
            dma((4,)),
            dma((chips,)), dma((chips,)),
            dma((nz,)), dma((nz,)),
            dma((chips,)), dma((chips,)),
            dma((chips,)), dma((chips,)),
            dma((chips,)), dma((chips,)),
        ],
        compiler_params=pltpu.CompilerParams(
            collective_id=0, has_side_effects=True, vmem_limit_bytes=VMEM_BYTES
        ),
        name="contrastive_step",
    )(
        pair_tokens.reshape(TOK, D),
        expert_ids.reshape(TOK, 2).T,
        positive.reshape(1, -1),
        w_router.T,
        w_qkv,
        w_out,
        w_up[0],
        w_down[0],
    )
    return (grad_up[None], grad_down[None])


def solution(mesh):
    return jax.shard_map(
        body,
        mesh=mesh,
        in_specs=(
            P(("wide", "narrow"), None, None, None),
            P(("wide", "narrow"), None, None),
            P(),
            P(),
            P(),
            P(),
            P("wide", None, "narrow"),
            P("wide", "narrow", None),
        ),
        out_specs=(P("wide", None, "narrow"), P("wide", "narrow", None)),
        check_vma=False,
    )
```
